256 devices in a mesh: gx: 16 (over z_lo, y, core), gy: 4 (over z_hi), gz: 4 (over x).
Axes of the slice: x: 4, y: 4, z: 8 (z_hi: 4, z_lo: 2; z = z_hi * 2 + z_lo), core: 2. Of those that a mesh axis runs over, the one named last changes fastest.
Arguments:
- positions: float32 [16, 4, 128, 3, 2, 128], P('gx', 'gy', 'gz'), may hold values from 0 to 1
- velocities: float32 [16, 4, 128, 3, 2, 128], P('gx', 'gy', 'gz'), may hold values from -6 to 6
- strength: float32 [16, 4, 128, 2, 128], P('gx', 'gy', 'gz'), may hold values from 0.05 to 0.4
- cluster_count: int32 [16, 4, 128], P('gx', 'gy', 'gz'), may hold values from 1 to 2, as said below
- migrant_ids: int32 [16, 4, 128, 1], P('gx', 'gy', 'gz'), may hold values from 0 to 1
- destination: int32 [16, 4, 128], replicated, may hold values from 0 to 5
- pair_i: int32 [16, 4, 128, 16], P('gx', 'gy', 'gz'), may hold values from 0 to 7
- pair_j: int32 [16, 4, 128, 16], P('gx', 'gy', 'gz'), may hold values from 0 to 111
- pair_count: int32 [16, 4, 128], P('gx', 'gy', 'gz'), may hold values from 4 to 16, as said below
Outputs:
- moved: float32 [16, 4, 128, 6, 8, 128], P('gx', 'gy', 'gz')
- forces: float32 [16, 4, 128, 3, 8, 128], P('gx', 'gy', 'gz')
The draws below stay inside these ranges and needn't reach their ends.
Inputs may be any that keep to these rules, and one draw needn't show every extreme that they name: `cluster_count`: some cell has all 2 slots occupied. `pair_count`: some cell has all 16 slots live.
All inputs are finite; a program needn't handle non-finite values.
Results may differ from the reference program's by a relative error of at most 0.0003.
Values sent between devices are 32-bit elements; how exact they have to be, the bound alone decides.
No kernel may reach another device: no remote copies, remote signals or barrier semaphores. Data moves between devices by JAX's collectives and lax.ppermute only.
A program may use at most 64 MiB of HBM per device.

```python
import math
import jax
import jax.numpy as jnp
from jax import lax

CL = 2
MIG = 1
PAIRS = 16
ATOMS = 128
NZ = 128
EXT = 8
PARTNERS = 112
N_GX = 16
N_GY = 4


def filled_counts(key, lowest, highest):
    first, second = jax.random.split(key)
    cells = N_GX * N_GY * NZ
    counts = jax.random.randint(first, (cells,), lowest, highest + 1)
    where = jax.random.randint(second, (), 0, cells)
    counts = jnp.where(jnp.arange(cells, dtype=jnp.int32) == where, highest, counts)
    return counts.reshape((N_GX, N_GY, NZ)).astype(jnp.int32)


def draw_cluster_count(key, part):
    key = jax.random.fold_in(key, 11)
    return filled_counts(key, CL // 2, CL)


def draw_pair_count(key, part):
    key = jax.random.fold_in(key, 13)
    return filled_counts(key, PAIRS // 4, PAIRS)


def plant(entries, key, low, high):
    spot = [jax.random.randint(jax.random.fold_in(key, axis), (), 0, length) for axis, length in enumerate(entries.shape)]
    widest = entries.shape.index(max(entries.shape))
    beside = spot[:widest] + [(spot[widest] + 1) % entries.shape[widest]] + spot[widest + 1:]
    return entries.at[tuple(spot)].set(low).at[tuple(beside)].set(high)


def steps_of(own_key, dims, pieces, low, largest):
    factor_of, own = 1.0, jax.random.fold_in(own_key, 6)
    for axis_at, shards_of in pieces:
        heights = jnp.exp(jax.random.uniform(jax.random.fold_in(own, axis_at), (shards_of,), jnp.float32, low / len(pieces), largest / len(pieces)))
        factor_of = factor_of * jnp.repeat(heights, dims[axis_at] // shards_of).reshape([-1 if axis == axis_at else 1 for axis in range(len(dims))])
    return factor_of


def gaussian(stream_key, dims, spread, most, cuts=(), kind=jnp.bfloat16):
    drawn = jax.random.normal(stream_key, dims, jnp.float32) * spread
    if len(cuts) > 0:
        drawn = steps_of(stream_key, dims, cuts, -0.22, 0.18) * drawn
    return jnp.clip(drawn, min=-most, max=most).astype(kind)


def setup_inputs(seed: int = 0) -> dict:
    streams_of = jax.random.split(jax.random.key(seed), 10)
    return {
        "positions": jnp.clip(1.0 * jax.random.uniform(streams_of[0], (N_GX, N_GY, NZ, 3, CL, ATOMS), jnp.float32) ** steps_of(streams_of[0], (N_GX, N_GY, NZ, 3, CL, ATOMS), ((0, 16), (1, 4), (2, 4)), -0.2, 0.2), 0.0, 1.0),
        "velocities": gaussian(streams_of[1], (N_GX, N_GY, NZ, 3, CL, ATOMS), 1.0, 6.0, ((0, 16), (1, 4), (2, 4)), jnp.float32),
        "strength": jnp.clip(jnp.exp(math.log(0.4) - 2.0794415 * jax.random.uniform(streams_of[2], (N_GX, N_GY, NZ, CL, ATOMS), jnp.float32) ** steps_of(streams_of[2], (N_GX, N_GY, NZ, CL, ATOMS), ((0, 16), (1, 4), (2, 4)), -0.2, 0.2)), 0.05, 0.4),
        "cluster_count": draw_cluster_count(jax.random.fold_in(streams_of[9], 71), 0),
        "migrant_ids": plant(jax.random.randint(streams_of[4], (N_GX, N_GY, NZ, MIG), 0, CL), jax.random.fold_in(streams_of[4], 1), 0, CL - 1).astype(jnp.int32),
        "destination": plant(jax.random.randint(streams_of[5], (N_GX, N_GY, NZ), 0, 6), jax.random.fold_in(streams_of[5], 1), 0, 5).astype(jnp.int32),
        "pair_i": plant(jax.random.randint(streams_of[6], (N_GX, N_GY, NZ, PAIRS), 0, EXT), jax.random.fold_in(streams_of[6], 1), 0, EXT - 1).astype(jnp.int32),
        "pair_j": plant(jax.random.randint(streams_of[7], (N_GX, N_GY, NZ, PAIRS), 0, PARTNERS), jax.random.fold_in(streams_of[7], 1), 0, PARTNERS - 1).astype(jnp.int32),
        "pair_count": draw_pair_count(jax.random.fold_in(streams_of[9], 71), 0),
    }


FACES = ((-1, 0, 0), (1, 0, 0), (0, -1, 0), (0, 1, 0), (0, 0, -1), (0, 0, 1))
SHELL = ((0, 0, 0), (0, 0, 1), (0, 1, -1), (0, 1, 0), (0, 1, 1), (1, -1, -1), (1, -1, 0), (1, -1, 1), (1, 0, -1), (1, 0, 0), (1, 0, 1), (1, 1, -1), (1, 1, 0), (1, 1, 1))
STEP = 0.01
SOFTEN = 0.1


def neighbour(field, offset):
    return jnp.roll(field, (-offset[0], -offset[1], -offset[2]), axis=(0, 1, 2))


def move_frame(field, offset):
    rows = field.shape[3]
    vector = jnp.array([float(offset[0]), float(offset[1]), float(offset[2])] + [0.0] * (rows - 3), dtype=jnp.float32)
    return field + vector.reshape((1, 1, 1, rows, 1, 1))


def cell_forces(inputs):
    coords, partners, first, second, live_count = inputs
    left = jnp.take(coords, first, axis=1)
    right = jnp.take(partners, second, axis=1)
    diff = left[0:3, :, :, None] - right[0:3, :, None, :]
    dist = jnp.sum(diff * diff, axis=0)
    reach = jnp.maximum(1.0 - dist, 0.0)
    lower = jnp.arange(ATOMS, dtype=jnp.int32)[:, None] < jnp.arange(ATOMS, dtype=jnp.int32)[None, :]
    live = jnp.arange(PAIRS, dtype=jnp.int32) < live_count
    same = (first == second)[:, None, None]
    allowed = live[:, None, None] & (jnp.logical_not(same) | lower[None])
    weight = jnp.where(allowed, left[3][:, :, None] * right[3][:, None, :] * reach * reach / (dist + SOFTEN), 0.0)
    push = weight[None] * diff
    on_left = jnp.sum(push, axis=3)
    on_right = -jnp.sum(push, axis=2)
    own = jax.ops.segment_sum(jnp.moveaxis(on_left, 1, 0), first, num_segments=EXT)
    other = jax.ops.segment_sum(jnp.moveaxis(on_right, 1, 0), second, num_segments=PARTNERS)
    return jnp.moveaxis(own, 0, 1), jnp.moveaxis(other, 0, 1)


def reference(positions, velocities, strength, cluster_count, migrant_ids, destination, pair_i, pair_j, pair_count):
    state = jnp.concatenate([positions, velocities, strength[:, :, :, None]], axis=3)
    slots = jnp.arange(CL, dtype=jnp.int32)
    leaving = jnp.any(slots[None, None, None, :, None] == migrant_ids[:, :, :, None, :], axis=4)
    keep = ((slots[None, None, None, :] < cluster_count[:, :, :, None]) & jnp.logical_not(leaving)).astype(jnp.float32)
    staying = state * keep[:, :, :, None, :, None]
    index = jnp.broadcast_to(migrant_ids[:, :, :, None, :, None], (N_GX, N_GY, NZ, 7, MIG, ATOMS))
    filled = (migrant_ids < cluster_count[:, :, :, None]).astype(jnp.float32)
    outgoing = jnp.take_along_axis(state, index, axis=4) * filled[:, :, :, None, :, None]
    inbox = []
    for face in range(6):
        offset = FACES[face]
        piece = neighbour(outgoing, offset)
        heading = neighbour(destination, offset)
        valid = (heading == face).astype(jnp.float32)
        inbox.append(move_frame(piece, offset) * valid[:, :, :, None, None, None])
    extended = jnp.concatenate([staying] + inbox, axis=4)
    coords = jnp.concatenate([extended[:, :, :, 0:3], extended[:, :, :, 6:7]], axis=3)
    partners = jnp.concatenate([move_frame(neighbour(coords, offset), offset) for offset in SHELL], axis=4)
    cells = N_GX * N_GY * NZ
    own, other = lax.map(cell_forces, (coords.reshape((cells, 4, EXT, ATOMS)), partners.reshape((cells, 4, PARTNERS, ATOMS)), pair_i.reshape((cells, PAIRS)), pair_j.reshape((cells, PAIRS)), pair_count.reshape((cells,))))
    own = own.reshape((N_GX, N_GY, NZ, 3, EXT, ATOMS))
    other = other.reshape((N_GX, N_GY, NZ, 3, 14, EXT, ATOMS))
    forces = own + other[:, :, :, :, 0]
    for block in range(1, 14):
        offset = SHELL[block]
        forces = forces + neighbour(other[:, :, :, :, block], (-offset[0], -offset[1], -offset[2]))
    new_velocity = extended[:, :, :, 3:6] + STEP * forces
    new_position = extended[:, :, :, 0:3] + STEP * new_velocity
    moved = jnp.concatenate([new_position, new_velocity], axis=3)
    return moved, forces
```

```python
import numpy as np
import jax
import jax.numpy as jnp
from jax import lax
from jax.experimental import pallas as pl
from jax.experimental.pallas import tpu as pltpu
from jax.sharding import PartitionSpec as P

FACES = ((-1, 0, 0), (1, 0, 0), (0, -1, 0), (0, 1, 0), (0, 0, -1), (0, 0, 1))
SHELL = (
    (0, 0, 0),
    (0, 0, 1),
    (0, 1, -1),
    (0, 1, 0),
    (0, 1, 1),
    (1, -1, -1),
    (1, -1, 0),
    (1, -1, 1),
    (1, 0, -1),
    (1, 0, 0),
    (1, 0, 1),
    (1, 1, -1),
    (1, 1, 0),
    (1, 1, 1),
)
STEP = 0.01
SOFTEN = 0.1
CELLS = 32
ATOMS = 128
PAIRS = 16
NX, NY = 16, 4
LANES = 128
ROW_LIVE, ROW_MIG, ROW_COUNT = 32, 33, 34
TABLE = 40
HALO = 32
HX = HALO + TABLE
BEHIND = ((0, 0), (0, -1), (-1, 1), (-1, 0), (-1, -1))
NEAR = tuple((dx, dy) for dx in (-1, 0, 1) for dy in (-1, 0, 1))
MAX_TASKS = CELLS * PAIRS + len(BEHIND) * (CELLS + 2) * PAIRS

SMEM = pltpu.SMEM
VMEM = pltpu.VMEM
f32 = jnp.float32
i32 = jnp.int32

BUFFERS = (
    ("own", 352), ("S_p", 128), ("S_m", 128), ("O_p", 128), ("O_m", 128), ("O_2", 128),
    ("HX_0", HX), ("HX_p", HX), ("HX_m", HX), ("HO_2", 16),
    ("own_xp", 352), ("OB_xp", 384), ("SB_xp", 256), ("HXB_xp", 3 * HX + 16),
    ("own_xm", 352), ("OB_xm", 384), ("SB_xm", 256), ("HXB_xm", 3 * HX + 16),
    ("O_xpp", 128), ("OC_xpp", 256), ("HOC_xpp", 48),
    ("O_xmm", 128), ("OC_xmm", 256), ("HOC_xmm", 48),
)
BASE = {}
_at = 0
for _name, _rows in BUFFERS:
    BASE[_name] = _at
    _at += _rows
POOL_ROWS = _at


def cluster_tables():
    base = np.zeros((5, 5, 2), np.int32)
    halo = np.zeros((5, 5, 2), np.int32)

    def put(dx, dy, stay, out, hstay, hout):
        base[dx + 2, dy + 2] = (stay, out)
        halo[dx + 2, dy + 2] = (hstay, hout)

    b = BASE
    put(0, 0, b["own"], b["own"] + 128, b["HX_0"], b["HX_0"] + 16)
    put(0, 1, b["S_p"], b["O_p"], b["HX_p"], b["HX_p"] + 16)
    put(0, -1, b["S_m"], b["O_m"], b["HX_m"], b["HX_m"] + 16)
    for dy in (-2, 2):
        put(0, dy, 0, b["O_2"], 0, b["HO_2"])
    for dx, s in ((1, "_xp"), (-1, "_xm")):
        h = b["HXB" + s]
        put(dx, 0, b["own" + s], b["own" + s] + 128, h, h + 16)
        put(dx, 1, b["SB" + s], b["OB" + s], h + HX, h + HX + 16)
        put(dx, -1, b["SB" + s] + 128, b["OB" + s] + 128, h + 2 * HX, h + 2 * HX + 16)
        for dy in (-2, 2):
            put(dx, dy, 0, b["OB" + s] + 256, 0, h + 3 * HX)
    for dx, s in ((2, "_xpp"), (-2, "_xmm")):
        put(dx, 0, 0, b["O" + s], 0, b["HOC" + s])
        put(dx, 1, 0, b["OC" + s], 0, b["HOC" + s] + 16)
        put(dx, -1, 0, b["OC" + s] + 128, 0, b["HOC" + s] + 32)
    assert np.all(base % 4 == 0) and np.all(halo % 4 == 0)
    shell = np.array(SHELL, np.int32).reshape(-1)
    faces = np.array(((0, 0, 0), (0, 0, 0)) + FACES, np.int32).reshape(-1)
    return np.concatenate([shell, faces, base.reshape(-1) // 4, halo.reshape(-1) // 4])


T_FACE = 42
T_BASE = T_FACE + 24
T_HALO = T_BASE + 50


def moved_by(array, axis, by):
    size = lax.axis_size(axis)
    return lax.ppermute(array, axis, [(i, (i + by) % size) for i in range(size)])


def pack_kernel(pos, stren, vel, meta, own, stay_ref, out_ref, vout_ref, low, high):
    ids = jnp.broadcast_to(meta[:, ROW_MIG : ROW_MIG + 1], (CELLS, LANES))
    count = jnp.broadcast_to(meta[:, ROW_COUNT : ROW_COUNT + 1], (CELLS, LANES))
    first = ids == 0.0
    kept = (1.0 - ids) < count
    filled = ids < count
    for c in range(4):
        if c < 3:
            one = pos[pl.ds(2 * c, CELLS, stride=6), :]
            two = pos[pl.ds(2 * c + 1, CELLS, stride=6), :]
        else:
            one = stren[pl.ds(0, CELLS, stride=2), :]
            two = stren[pl.ds(1, CELLS, stride=2), :]
        stay_ref[pl.ds(c, CELLS, stride=4), :] = jnp.where(kept, jnp.where(first, two, one), 0.0)
        out_ref[pl.ds(c, CELLS, stride=4), :] = jnp.where(filled, jnp.where(first, one, two), 0.0)
    for c in range(3):
        one = vel[pl.ds(2 * c, CELLS, stride=6), :]
        two = vel[pl.ds(2 * c + 1, CELLS, stride=6), :]
        vout_ref[pl.ds(c, CELLS, stride=3), :] = jnp.where(filled, jnp.where(first, one, two), 0.0)
    own[0:128, :] = stay_ref[...]
    own[128:256, :] = out_ref[...]
    own[256:352, :] = vout_ref[...]
    full = jnp.concatenate([meta[...], jnp.zeros((LANES - CELLS, LANES), f32)], axis=0)
    table = full.T[0:TABLE, :]
    low[0:8, :] = stay_ref[0:8, :]
    low[8:16, :] = out_ref[0:8, :]
    low[16:24, :] = vout_ref[0:8, :]
    low[24:64, :] = table
    high[0:8, :] = stay_ref[120:128, :]
    high[8:16, :] = out_ref[120:128, :]
    high[16:24, :] = vout_ref[88:96, :]
    high[24:64, :] = table


def place():
    return lax.axis_index("gx"), lax.axis_index("gy"), lax.axis_index("gz")


def heading_row(dest, x, y, dx, dy):
    row = lax.rem(x + (dx + NX), NX) * NY + lax.rem(y + (dy + NY), NY)
    return dest[pl.ds(row, 1), :]


def z_shift(z):
    return lax.rem(LANES + 2 - z * CELLS, LANES)


def flags_kernel(dest, hx0, hxp, hxm, hxbp, hxbm, masks, codes, heads, occ, turn):
    x, y, z = place()
    heads[...] = jnp.zeros_like(heads)
    for dx in range(-2, 3):
        for dy in range(-2, 3):
            if abs(dx) + abs(dy) < 4:
                at = (dx + 2) * 5 + dy + 2
                heads[at : at + 1, :] = heading_row(dest, x, y, dx, dy)
    heads[...] = pltpu.roll(heads[...], z_shift(z), 1)

    def head(dx, dy):
        at = (dx + 2) * 5 + dy + 2
        return heads[at : at + 1, :]

    tables = {
        (0, 0): (hx0, 0), (0, 1): (hxp, 0), (0, -1): (hxm, 0),
        (1, 0): (hxbp, 0), (1, 1): (hxbp, HX), (1, -1): (hxbp, 2 * HX),
        (-1, 0): (hxbm, 0), (-1, 1): (hxbm, HX), (-1, -1): (hxbm, 2 * HX),
    }

    def rows(column, first, many):
        ref, at = tables[column]
        at = at + HALO + first
        return ref[at : at + many, :].astype(i32)

    one = jnp.ones((1, LANES), i32)
    ids = {c: rows(c, ROW_MIG, 1) for c in NEAR}
    counts = {c: rows(c, ROW_COUNT, 1) for c in NEAR}
    filled = {c: (ids[c] < counts[c]).astype(i32) for c in NEAR}

    def coming(dx, dy, face):
        return (head(dx, dy) == face).astype(i32) * filled.get((dx, dy), one)

    occ[...] = jnp.zeros_like(occ)
    turn[...] = jnp.zeros_like(turn)
    for n, (dx, dy) in enumerate(NEAR):
        turn[n : n + 1, :] = coming(dx, dy, 4) * 64
        turn[16 + n : 17 + n, :] = coming(dx, dy, 5) * 128
    from_below = pltpu.roll(turn[0:16, :], 1, 1)
    from_above = pltpu.roll(turn[16:32, :], LANES - 1, 1)
    for n, (dx, dy) in enumerate(NEAR):
        c = (dx, dy)
        kept0 = ((counts[c] > 0) & (ids[c] != 0)).astype(i32)
        kept1 = ((counts[c] > 1) & (ids[c] != 1)).astype(i32)
        sides = (
            coming(dx - 1, dy, 0) * 4
            + coming(dx + 1, dy, 1) * 8
            + coming(dx, dy - 1, 2) * 16
            + coming(dx, dy + 1, 3) * 32
        )
        occ[n : n + 1, :] = kept0 + 2 * kept1 + sides
    here = occ[...] + from_below + from_above
    by_z = {0: here, 1: pltpu.roll(here, LANES - 1, 1), -1: pltpu.roll(here, 1, 1)}

    def occupied(column, dz):
        n = NEAR.index(column)
        return jnp.broadcast_to(by_z[dz][n : n + 1, :], (PAIRS, LANES))

    slot = lax.broadcasted_iota(i32, (PAIRS, LANES), 0)
    lane = lax.broadcasted_iota(i32, (PAIRS, LANES), 1)
    masks[...] = jnp.zeros_like(masks)
    for g, column in enumerate(BEHIND):
        first = rows(column, 0, PAIRS)
        second = rows(column, PAIRS, PAIRS)
        live = slot < rows(column, ROW_LIVE, 1)
        block = lax.shift_right_logical(second, 3)
        part = second & 7
        there = live & ((lax.shift_right_logical(occupied(column, 0), first) & 1) == 1)
        codes[PAIRS * g : PAIRS * (g + 1), :] = first + 8 * second
        if g == 0:
            left = jnp.zeros((PAIRS, LANES), i32)
            for b, (ox, oy, oz) in enumerate(SHELL):
                bit = lax.shift_right_logical(occupied((ox, oy), oz), part) & 1
                left = jnp.where(block == b, bit, left)
            keep = there & (left == 1) & (lane >= 2) & (lane < CELLS + 2)
            word = jnp.where(keep, lax.shift_left(jnp.ones_like(slot), slot), 0)
            masks[0:1, :] = jnp.sum(word, axis=0, keepdims=True)
        right = jnp.zeros((PAIRS, LANES), i32)
        for b, (ox, oy, oz) in enumerate(SHELL):
            if (ox, oy) == (-column[0], -column[1]):
                bit = lax.shift_right_logical(occupied((0, 0), oz), part) & 1
                inside = (lane + oz >= 2) & (lane + oz < CELLS + 2)
                right = jnp.where((block == b) & inside, bit, right)
        keep = there & (right == 1) & (first != second)
        word = jnp.where(keep, lax.shift_left(jnp.ones_like(slot), slot), 0)
        masks[1 + g : 2 + g, :] = jnp.sum(word, axis=0, keepdims=True)


def list_kernel(table, masks, codes, tasks):
    tasks[0] = 0

    def add(left, lane, code):
        first = code & 7
        block = lax.shift_right_logical(code, 6)
        part = lax.shift_right_logical(code, 3) & 7
        ox, oy, oz = (table[3 * block + a] for a in range(3))
        if left:
            mine, theirs, at = first, part, lane + oz
            target = lane - 2
        else:
            mine, theirs, at = part, first, lane
            target = lane + oz - 2
            ox, oy, oz = -ox, -oy, -oz
        fx, fy, fz = (table[T_FACE + 3 * theirs + a] for a in range(3))
        vx, vy, vz = ox + fx, oy + fy, oz + fz
        at = at + fz
        half = (theirs >= 2).astype(i32)
        which = ((vx + 2) * 5 + vy + 2) * 2 + half
        inner = table[T_BASE + which] + at - 2
        outer = table[T_HALO + which] + jnp.where(at < 2, at, at - CELLS)
        entry = jnp.where((at >= 2) & (at < CELLS + 2), inner, outer)
        n = tasks[0] + 1
        tasks[0] = n
        tasks[n] = (
            entry
            + (target * 8 + mine) * 2048
            + ((vx + 2) + 8 * (vy + 2) + 64 * (vz + 2)) * (2048 * 256)
        )

    for row in range(6):
        group = max(row - 1, 0)

        def lane_step(lane, _, row=row, group=group):
            mask = masks[row, lane]

            @pl.when(mask != 0)
            def _():
                def bit_step(p, _):
                    @pl.when((lax.shift_right_logical(mask, p) & 1) == 1)
                    def _():
                        add(row == 0, lane, codes[PAIRS * group + p, lane])

                    return 0

                lax.fori_loop(0, PAIRS, bit_step, 0)

            return 0

        lax.fori_loop(1, CELLS + 3, lane_step, 0)


def extend_kernel(dest, meta, vel, own, own_xp, own_xm, op, om, vp, vm, zlo, zhi, ext, heads):
    x, y, z = place()
    heads[...] = jnp.zeros_like(heads)
    spots = ((-1, 0), (1, 0), (0, -1), (0, 1), (0, 0))
    for n, (dx, dy) in enumerate(spots):
        heads[n : n + 1, :] = heading_row(dest, x, y, dx, dy)
    turned = pltpu.roll(heads[...], z_shift(z), 1)
    heads[...] = turned
    heads[5:6, :] = pltpu.roll(turned, LANES - 1, 1)[4:5, :]
    heads[4:5, :] = pltpu.roll(turned, 1, 1)[4:5, :]
    column = lax.broadcasted_iota(i32, (8, LANES), 0)
    valid = (heads[0:8, :] == column).astype(f32)
    full = jnp.concatenate([valid, jnp.zeros((LANES - 8, LANES), f32)], axis=0).T
    ids = jnp.broadcast_to(meta[:, ROW_MIG : ROW_MIG + 1], (CELLS, LANES))
    count = jnp.broadcast_to(meta[:, ROW_COUNT : ROW_COUNT + 1], (CELLS, LANES))
    for s in range(2):
        keep = (count > float(s)) & (ids != float(s))
        for r in range(7):
            if r < 3:
                value = own[pl.ds(r, CELLS, stride=4), :]
            elif r == 6:
                value = own[pl.ds(3, CELLS, stride=4), :]
            else:
                value = vel[pl.ds(2 * (r - 3) + s, CELLS, stride=6), :]
            ext[pl.ds(8 * r + s, CELLS, stride=56), :] = jnp.where(keep, value, 0.0)
    lateral = (
        (own_xm, 128, own_xm, 256),
        (own_xp, 128, own_xp, 256),
        (om, 0, vm, 0),
        (op, 0, vp, 0),
    )
    for f in range(6):
        flag = jnp.broadcast_to(full[2 : 2 + CELLS, f : f + 1], (CELLS, LANES))
        for r in range(7):
            shift = float(FACES[f][r]) if r < 3 else 0.0
            speed = 3 <= r < 6
            step = 3 if speed else 4
            row = r - 3 if speed else min(r, 3)
            if f < 4:
                place_ref, place_at, speed_ref, speed_at = lateral[f]
                ref, at = (speed_ref, speed_at) if speed else (place_ref, place_at)
                value = (ref[pl.ds(at + row, CELLS, stride=step), :] + shift) * flag
                ext[pl.ds(8 * r + 2 + f, CELLS, stride=56), :] = value
            else:
                at = 256 if speed else 128
                inner = CELLS - 1
                if f == 4:
                    value = own[pl.ds(at + row, inner, stride=step), :]
                    value = (value + shift) * flag[1:CELLS, :]
                    ext[pl.ds(56 + 8 * r + 6, inner, stride=56), :] = value
                    edge_row = (16 + 5 + row) if speed else 12 + row
                    edge = (zlo[edge_row : edge_row + 1, :] + shift) * flag[0:1, :]
                    ext[8 * r + 6 : 8 * r + 7, :] = edge
                else:
                    value = own[pl.ds(at + step + row, inner, stride=step), :]
                    value = (value + shift) * flag[0:inner, :]
                    ext[pl.ds(8 * r + 7, inner, stride=56), :] = value
                    edge_row = (16 + row) if speed else 8 + row
                    edge = (zhi[edge_row : edge_row + 1, :] + shift) * flag[inner:CELLS, :]
                    last = 56 * inner + 8 * r + 7
                    ext[last : last + 1, :] = edge


def force_kernel(tasks, ext, *refs):
    count = len(BUFFERS)
    buffers, (moved, forces, pool, sems) = refs[:count], refs[count:]
    copies = []
    for n, (name, size) in enumerate(BUFFERS):
        copies.append(
            pltpu.make_async_copy(
                buffers[n], pool.at[pl.ds(BASE[name], size), :], sems.at[n]
            )
        )
    for copy in copies:
        copy.start()
    forces[...] = jnp.zeros_like(forces)
    for copy in copies:
        copy.wait()

    def spread(row):
        wide = jnp.broadcast_to(pool[pl.ds(row, 1), :], (8, LANES))
        return pltpu.roll(wide, 0, 1, stride=1, stride_axis=0)

    def step(t, _):
        code = tasks[t + 1]
        row = (code & 2047) * 4
        target = lax.shift_right_logical(code, 11) & 255
        cell = lax.shift_right_logical(target, 3)
        slot = target & 7
        away = lax.shift_right_logical(code, 19)
        sx, sy, sz, ss = (spread(row + a) for a in range(4))
        ts = ext[cell, 6, pl.ds(slot, 1), :]
        goal = []
        for a in range(3):
            shift = ((lax.shift_right_logical(away, 3 * a) & 7) - 2).astype(f32)
            wide = jnp.broadcast_to(ext[cell, a, pl.ds(slot, 1), :], (8, LANES))
            goal.append(wide - shift)
        tx, ty, tz = goal
        fx = jnp.zeros((8, LANES), f32)
        fy, fz = fx, fx
        for j in range(LANES // 8):
            dx = tx - (pltpu.roll(sx, 8 * j, 1) if j else sx)
            dy = ty - (pltpu.roll(sy, 8 * j, 1) if j else sy)
            dz = tz - (pltpu.roll(sz, 8 * j, 1) if j else sz)
            strong = pltpu.roll(ss, 8 * j, 1) if j else ss
            dist = dx * dx + dy * dy + dz * dz
            reach = jnp.maximum(1.0 - dist, 0.0)
            weight = strong * reach * reach / (dist + SOFTEN)
            fx = fx + weight * dx
            fy = fy + weight * dy
            fz = fz + weight * dz
        for a, part in enumerate((fx, fy, fz)):
            total = jnp.sum(part, axis=0, keepdims=True) * ts
            forces[0, 0, cell, a, pl.ds(slot, 1), :] += total
        return 0

    lax.fori_loop(0, tasks[0], step, 0)

    def finish(cell, _):
        for a in range(3):
            speed = ext[cell, 3 + a] + STEP * forces[0, 0, cell, a]
            moved[0, 0, cell, 3 + a] = speed
            moved[0, 0, cell, a] = ext[cell, a] + STEP * speed
        return 0

    lax.fori_loop(0, CELLS, finish, 0)


def whole(space=VMEM):
    return pl.BlockSpec(memory_space=space)


def rows_of(n, dtype=f32):
    return jax.ShapeDtypeStruct((n, LANES), dtype)


def limit(mib):
    return pltpu.CompilerParams(vmem_limit_bytes=mib * 2**20)


def per_device(
    positions,
    velocities,
    strength,
    cluster_count,
    migrant_ids,
    destination,
    pair_i,
    pair_j,
    pair_count,
):
    pos = positions.reshape((CELLS * 6, ATOMS))
    vel = velocities.reshape((CELLS * 6, ATOMS))
    stren = strength.reshape((CELLS * 2, ATOMS))
    dest = destination.reshape((NX * NY, LANES))
    meta = jnp.concatenate(
        [
            pair_i[0, 0],
            pair_j[0, 0],
            pair_count.reshape((CELLS, 1)),
            migrant_ids.reshape((CELLS, 1)),
            cluster_count.reshape((CELLS, 1)),
            jnp.zeros((CELLS, LANES - 35), i32),
        ],
        axis=1,
    ).astype(f32)
    own, S, O, V, low, high = pl.pallas_call(
        pack_kernel,
        out_shape=[rows_of(352), rows_of(128), rows_of(128), rows_of(96), rows_of(64), rows_of(64)],
        in_specs=[whole()] * 4,
        out_specs=[whole()] * 6,
        compiler_params=limit(16),
        name="pack",
    )(pos, stren, vel, meta)

    cat = jnp.concatenate
    zlo = moved_by(high, "gz", 1)
    zhi = moved_by(low, "gz", -1)
    O_p, O_m, O_2 = moved_by(O, "gy", -1), moved_by(O, "gy", 1), moved_by(O, "gy", 2)
    S_p, S_m = moved_by(S, "gy", -1), moved_by(S, "gy", 1)
    own_xp, own_xm = moved_by(own, "gx", -1), moved_by(own, "gx", 1)
    O_xpp, O_xmm = moved_by(O, "gx", -2), moved_by(O, "gx", 2)
    table = cat(
        [zlo[24:64, 30:32], low[24:64, 0:32], zhi[24:64, 0:2], jnp.zeros((TABLE, 92), f32)], axis=1
    )
    HX_0 = cat([zlo[0:8], zhi[0:8], zlo[8:16], zhi[8:16], table], axis=0)
    HX_p, HX_m = moved_by(HX_0, "gy", -1), moved_by(HX_0, "gy", 1)
    HO_0 = HX_0[16:32]
    HO_2 = moved_by(HO_0, "gy", 2)
    V_p, V_m = moved_by(V, "gy", -1), moved_by(V, "gy", 1)
    OB = cat([O_p, O_m, O_2], axis=0)
    OC = cat([O_p, O_m], axis=0)
    SB = cat([S_p, S_m], axis=0)
    HXB = cat([HX_0, HX_p, HX_m, HO_2], axis=0)
    HOC = cat([HO_0, HX_p[16:32], HX_m[16:32]], axis=0)
    HXB_xp, HXB_xm = moved_by(HXB, "gx", -1), moved_by(HXB, "gx", 1)
    OB_xp, OB_xm = moved_by(OB, "gx", -1), moved_by(OB, "gx", 1)
    OC_xpp, OC_xmm = moved_by(OC, "gx", -2), moved_by(OC, "gx", 2)
    HOC_xpp, HOC_xmm = moved_by(HOC, "gx", -2), moved_by(HOC, "gx", 2)
    SB_xp, SB_xm = moved_by(SB, "gx", -1), moved_by(SB, "gx", 1)

    masks, codes = pl.pallas_call(
        flags_kernel,
        out_shape=[rows_of(8, i32), rows_of(PAIRS * len(BEHIND), i32)],
        in_specs=[whole()] * 6,
        out_specs=[whole()] * 2,
        scratch_shapes=[VMEM((32, LANES), i32), VMEM((16, LANES), i32), VMEM((32, LANES), i32)],
        compiler_params=limit(8),
        name="flags",
    )(dest, HX_0, HX_p, HX_m, HXB_xp, HXB_xm)
    tasks = pl.pallas_call(
        list_kernel,
        out_shape=jax.ShapeDtypeStruct((MAX_TASKS + 16,), i32),
        in_specs=[whole(SMEM)] * 3,
        out_specs=whole(SMEM),
        name="list",
    )(jnp.asarray(cluster_tables()), masks, codes)
    ext = pl.pallas_call(
        extend_kernel,
        out_shape=rows_of(CELLS * 56),
        in_specs=[whole()] * 12,
        out_specs=whole(),
        scratch_shapes=[VMEM((8, LANES), i32)],
        compiler_params=limit(16),
        name="extend",
    )(dest, meta, vel, own, own_xp, own_xm, O_p, O_m, V_p, V_m, zlo, zhi)

    values = dict(
        own=own, S_p=S_p, S_m=S_m, O_p=O_p, O_m=O_m, O_2=O_2,
        HX_0=HX_0, HX_p=HX_p, HX_m=HX_m, HO_2=HO_2,
        own_xp=own_xp, OB_xp=OB_xp, SB_xp=SB_xp, HXB_xp=HXB_xp,
        own_xm=own_xm, OB_xm=OB_xm, SB_xm=SB_xm, HXB_xm=HXB_xm,
        O_xpp=O_xpp, OC_xpp=OC_xpp, HOC_xpp=HOC_xpp,
        O_xmm=O_xmm, OC_xmm=OC_xmm, HOC_xmm=HOC_xmm,
    )
    return pl.pallas_call(
        force_kernel,
        out_shape=[
            jax.ShapeDtypeStruct((1, 1, CELLS, 6, 8, LANES), f32),
            jax.ShapeDtypeStruct((1, 1, CELLS, 3, 8, LANES), f32),
        ],
        in_specs=[whole(SMEM), whole()] + [whole(pl.ANY)] * len(BUFFERS),
        out_specs=[whole()] * 2,
        scratch_shapes=[
            VMEM((POOL_ROWS, LANES), f32),
            pltpu.SemaphoreType.DMA((len(BUFFERS),)),
        ],
        compiler_params=limit(24),
        name="forces",
    )(tasks, ext.reshape((CELLS, 7, 8, LANES)), *[values[name] for name, _ in BUFFERS])


def solution(mesh):
    in_specs = (
        P("gx", "gy", "gz", None, None, None),
        P("gx", "gy", "gz", None, None, None),
        P("gx", "gy", "gz", None, None),
        P("gx", "gy", "gz"),
        P("gx", "gy", "gz", None),
        P(),
        P("gx", "gy", "gz", None),
        P("gx", "gy", "gz", None),
        P("gx", "gy", "gz"),
    )
    out_specs = (P("gx", "gy", "gz", None, None, None), P("gx", "gy", "gz", None, None, None))
    return jax.shard_map(
        per_device, mesh=mesh, in_specs=in_specs, out_specs=out_specs, check_vma=False
    )
```

```python
import numpy as np
import jax
import jax.numpy as jnp
from jax import lax
from jax.experimental import pallas as pl
from jax.experimental.pallas import tpu as pltpu
from jax.sharding import PartitionSpec as P

FACES = ((-1, 0, 0), (1, 0, 0), (0, -1, 0), (0, 1, 0), (0, 0, -1), (0, 0, 1))
SHELL = (
    (0, 0, 0),
    (0, 0, 1),
    (0, 1, -1),
    (0, 1, 0),
    (0, 1, 1),
    (1, -1, -1),
    (1, -1, 0),
    (1, -1, 1),
    (1, 0, -1),
    (1, 0, 0),
    (1, 0, 1),
    (1, 1, -1),
    (1, 1, 0),
    (1, 1, 1),
)
STEP = 0.01
SOFTEN = 0.1
CELLS = 32
WIDE = CELLS + 4
ATOMS = 128
PAIRS = 16
NX, NY = 16, 4
LANES = 128
SEG = 40
ROW_LIVE, ROW_MIG, ROW_COUNT = 0, 1, 2
BEHIND = ((0, 0), (0, -1), (-1, 1), (-1, 0), (-1, -1))
NEAR = tuple((dx, dy) for dx in (-1, 0, 1) for dy in (-1, 0, 1))
MAX_TASKS = CELLS * PAIRS + len(BEHIND) * (CELLS + 2) * PAIRS

SMEM = pltpu.SMEM
VMEM = pltpu.VMEM
f32 = jnp.float32
i32 = jnp.int32

AT_S, AT_O, AT_T, AT_V, BUNDLE = 0, 128, 256, 272, 368
SHORT = AT_V
X1 = BUNDLE + 2 * SHORT + 128
X2 = 384
P_B, P_BP, P_BM, P_O2 = 0, BUNDLE, 2 * BUNDLE, 3 * BUNDLE
P_XP = P_O2 + 128
P_XM = P_XP + X1
P_X2P = P_XM + X1
P_X2M = P_X2P + X2
POOL = P_X2M + X2


def column_rows():
    at = {(0, 0): P_B, (0, 1): P_BP, (0, -1): P_BM}
    for dy in (-2, 2):
        at[0, dy] = P_O2 - 128
    for dx, x1, x2 in ((1, P_XP, P_X2P), (-1, P_XM, P_X2M)):
        at[dx, 0] = x1
        at[dx, 1] = x1 + BUNDLE
        at[dx, -1] = x1 + BUNDLE + SHORT
        for dy in (-2, 2):
            at[dx, dy] = x1 + BUNDLE + 2 * SHORT - 128
        at[2 * dx, 0] = x2 - 128
        at[2 * dx, 1] = x2
        at[2 * dx, -1] = x2 + 128
    return at


COLUMN = column_rows()
FAR = tuple(c for c in ((0, 2), (1, 2), (-1, 2), (2, 0), (2, 1), (2, -1), (-2, 0), (-2, 1), (-2, -1)))
E_T = 16 * len(NEAR) + 8 * len(FAR)
E_V = E_T + 16
EDGE = E_V + 8
EDGE_AT = {c: 16 * n for n, c in enumerate(NEAR)}
for _n, _c in enumerate(FAR):
    EDGE_AT[_c] = 16 * len(NEAR) + 8 * _n - 8
    if _c[1] == 2:
        EDGE_AT[_c[0], -2] = EDGE_AT[_c]


def moved_by(array, axis, by):
    size = lax.axis_size(axis)
    return lax.ppermute(array, axis, [(i, (i + by) % size) for i in range(size)])


def to_column(rows):
    pad = jnp.zeros((LANES - rows.shape[0], LANES), f32)
    return jnp.concatenate([rows, pad], axis=0).T


def pack_kernel(pos, stren, vel, first, second, live, mig, count, bundle, out_ref):
    bundle[AT_T : AT_T + 16, :] = jnp.zeros((16, LANES), f32)
    bundle[AT_T : AT_T + 16, 2 : 2 + CELLS] = first[...].astype(f32)
    bundle[AT_T : AT_T + 16, SEG + 2 : SEG + 2 + CELLS] = second[...].astype(f32)
    low = 2 * SEG + 2
    for row, ref in ((ROW_LIVE, live), (ROW_MIG, mig), (ROW_COUNT, count)):
        bundle[AT_T + row : AT_T + row + 1, low : low + CELLS] = ref[...].astype(f32)
    turned = to_column(bundle[AT_T : AT_T + 8, :])[low : low + CELLS, :]
    ids = jnp.broadcast_to(turned[:, ROW_MIG : ROW_MIG + 1], (CELLS, LANES))
    many = jnp.broadcast_to(turned[:, ROW_COUNT : ROW_COUNT + 1], (CELLS, LANES))
    low_slot = ids == 0.0
    kept = (1.0 - ids) < many
    filled = ids < many
    for c in range(4):
        if c < 3:
            one = pos[pl.ds(2 * c, CELLS, stride=6), :]
            two = pos[pl.ds(2 * c + 1, CELLS, stride=6), :]
        else:
            one = stren[pl.ds(0, CELLS, stride=2), :]
            two = stren[pl.ds(1, CELLS, stride=2), :]
        stay = jnp.where(kept, jnp.where(low_slot, two, one), 0.0)
        out = jnp.where(filled, jnp.where(low_slot, one, two), 0.0)
        bundle[pl.ds(AT_S + c, CELLS, stride=4), :] = stay
        bundle[pl.ds(AT_O + c, CELLS, stride=4), :] = out
        out_ref[pl.ds(c, CELLS, stride=4), :] = out
    for c in range(3):
        one = vel[pl.ds(2 * c, CELLS, stride=6), :]
        two = vel[pl.ds(2 * c + 1, CELLS, stride=6), :]
        speed = jnp.where(filled, jnp.where(low_slot, one, two), 0.0)
        bundle[pl.ds(AT_V + c, CELLS, stride=3), :] = speed


def place():
    return lax.axis_index("gx"), lax.axis_index("gy"), lax.axis_index("gz")


def heading_row(dest, x, y, dx, dy):
    row = lax.rem(x + (dx + NX), NX) * NY + lax.rem(y + (dy + NY), NY)
    return dest[pl.ds(row, 1), :]


def z_shift(z):
    return lax.rem(LANES + 2 - z * CELLS, LANES)


def iota(shape, axis):
    return lax.broadcasted_iota(i32, shape, axis)


def edges_kernel(b, bp, bm, o2, xp, xm, x2p, x2m, low, high):
    parts = (
        (P_B, b), (P_BP, bp), (P_BM, bm), (P_O2, o2),
        (P_XP, xp), (P_XM, xm), (P_X2P, x2p), (P_X2M, x2m),
    )

    def find(row):
        for start, ref in reversed(parts):
            if row >= start:
                return ref, row - start

    lane = iota((16, LANES), 1)
    for side, ref, cell in ((0, low, 0), (1, high, CELLS - 2)):
        table = jnp.zeros((16, LANES), f32)
        for n, column in enumerate(NEAR):
            source, row = find(COLUMN[column])
            to = EDGE_AT[column]
            ref[to : to + 8, :] = source[row + 4 * cell : row + 4 * cell + 8, :]
            row = row + 128
            ref[to + 8 : to + 16, :] = source[row + 4 * cell : row + 4 * cell + 8, :]
            values = source[row + 128 : row + 144, :]
            rolled = pltpu.roll(values, (2 * n - 2 - cell) % LANES, 1)
            for s in range(3):
                here = (lane >= s * SEG + 2 * n) & (lane < s * SEG + 2 * n + 2)
                table = jnp.where(here, rolled, table)
        for column in FAR:
            source, row = find(COLUMN[column] + 128)
            to = EDGE_AT[column] + 8
            ref[to : to + 8, :] = source[row + 4 * cell : row + 4 * cell + 8, :]
        ref[E_T : E_T + 16, :] = table
        at = AT_V + (88 if side else 0)
        ref[E_V : E_V + 8, :] = b[at : at + 8, :]


def find_tasks(dest, pool, edges, masks, words, heads, occ, turn):
    x, y, z = place()
    heads[...] = jnp.zeros_like(heads)
    for dx in range(-2, 3):
        for dy in range(-2, 3):
            if abs(dx) + abs(dy) < 4:
                at = (dx + 2) * 5 + dy + 2
                heads[at : at + 1, :] = heading_row(dest, x, y, dx, dy)
    heads[...] = pltpu.roll(heads[...], z_shift(z), 1)

    def head(dx, dy):
        at = (dx + 2) * 5 + dy + 2
        return heads[at : at + 1, :]

    slot = iota((PAIRS, LANES), 0)
    lane = iota((PAIRS, LANES), 1)
    thin = iota((1, LANES), 1)
    tables = {}
    for n, column in enumerate(NEAR):
        row = COLUMN[column] + AT_T
        values = pool[row : row + 16, :]
        if edges is not None:
            zlo, zhi = edges
            below = pltpu.roll(zlo[E_T : E_T + 16, :], (-2 * n) % LANES, 1)
            above = pltpu.roll(zhi[E_T : E_T + 16, :], (34 - 2 * n) % LANES, 1)
            for s in range(3):
                values = jnp.where((lane >= s * SEG) & (lane < s * SEG + 2), below, values)
                values = jnp.where((lane >= s * SEG + 34) & (lane < s * SEG + 36), above, values)
        tables[column] = values.astype(i32)
    rest = {c: pltpu.roll(tables[c], LANES - 2 * SEG, 1) for c in NEAR}
    ids = {c: rest[c][ROW_MIG : ROW_MIG + 1, :] for c in NEAR}
    counts = {c: rest[c][ROW_COUNT : ROW_COUNT + 1, :] for c in NEAR}
    filled = {c: (ids[c] < counts[c]).astype(i32) for c in NEAR}
    if edges is None:
        default = ((thin >= 2) & (thin < CELLS + 2)).astype(i32)
    else:
        default = jnp.ones((1, LANES), i32)

    def coming(dx, dy, face):
        return (head(dx, dy) == face).astype(i32) * filled.get((dx, dy), default)

    occ[...] = jnp.zeros_like(occ)
    turn[...] = jnp.zeros_like(turn)
    for n, (dx, dy) in enumerate(NEAR):
        turn[n : n + 1, :] = coming(dx, dy, 4) * 64
        turn[16 + n : 17 + n, :] = coming(dx, dy, 5) * 128
    from_below = pltpu.roll(turn[0:16, :], 1, 1)
    from_above = pltpu.roll(turn[16:32, :], LANES - 1, 1)
    for n, (dx, dy) in enumerate(NEAR):
        c = (dx, dy)
        kept0 = ((counts[c] > 0) & (ids[c] != 0)).astype(i32)
        kept1 = ((counts[c] > 1) & (ids[c] != 1)).astype(i32)
        sides = (
            coming(dx - 1, dy, 0) * 4
            + coming(dx + 1, dy, 1) * 8
            + coming(dx, dy - 1, 2) * 16
            + coming(dx, dy + 1, 3) * 32
        )
        occ[n : n + 1, :] = kept0 + 2 * kept1 + sides
    here = occ[...] + from_below + from_above
    by_z = {0: here, 1: pltpu.roll(here, LANES - 1, 1), -1: pltpu.roll(here, 1, 1)}

    def occupied(column, dz):
        n = NEAR.index(column)
        return jnp.broadcast_to(by_z[dz][n : n + 1, :], (PAIRS, LANES))

    def face_of(k):
        fx = jnp.where(k == 3, 1, jnp.where(k == 2, -1, 0))
        fy = jnp.where(k == 5, 1, jnp.where(k == 4, -1, 0))
        fz = jnp.where(k == 7, 1, jnp.where(k == 6, -1, 0))
        return fx, fy, fz

    def word_of(mine, target, theirs, at, vx, vy, vz, columns):
        half = (theirs >= 2).astype(i32)
        which = (vx + 2) * 5 + vy + 2
        inner = jnp.zeros_like(slot)
        outer = jnp.zeros_like(slot)
        for cx, cy in columns:
            same = which == (cx + 2) * 5 + cy + 2
            inner = jnp.where(same, COLUMN[cx, cy] // 4, inner)
            if edges is not None:
                outer = jnp.where(same, EDGE_AT[cx, cy] // 4, outer)
        entry = inner + 32 * half + at - 2
        if edges is not None:
            low_edge = outer + 2 * half + at + POOL // 4
            high_edge = outer + 2 * half + at - 34 + (POOL + EDGE) // 4
            entry = jnp.where(at < 2, low_edge, jnp.where(at >= CELLS + 2, high_edge, entry))
        return (
            entry
            + (target * 8 + mine) * 2048
            + ((vx + 2) + 8 * (vy + 2) + 64 * (vz + 2)) * (2048 * 256)
        )

    masks[...] = jnp.zeros_like(masks)
    power = lax.shift_left(jnp.ones_like(slot), slot)
    for g, column in enumerate(BEHIND):
        cx, cy = column
        inside = lane < WIDE
        first = jnp.where(inside, tables[column], 0)
        second = jnp.where(inside, pltpu.roll(tables[column], LANES - SEG, 1), 0)
        live = inside & (slot < rest[column][ROW_LIVE : ROW_LIVE + 1, :])
        block = lax.shift_right_logical(second, 3)
        part = second & 7
        there = live & ((lax.shift_right_logical(occupied(column, 0), first) & 1) == 1)
        if g == 0:
            left = jnp.zeros((PAIRS, LANES), i32)
            bx, by, bz = left, left, left
            for b, (ox, oy, oz) in enumerate(SHELL):
                same = block == b
                bit = lax.shift_right_logical(occupied((ox, oy), oz), part) & 1
                left = jnp.where(same, bit, left)
                bx = jnp.where(same, ox, bx)
                by = jnp.where(same, oy, by)
                bz = jnp.where(same, oz, bz)
            keep = there & (left == 1) & (lane >= 2) & (lane < CELLS + 2)
            fx, fy, fz = face_of(part)
            words[0:PAIRS, :] = word_of(
                first, lane - 2, part, lane + bz + fz, bx + fx, by + fy, bz + fz, COLUMN
            )
            masks[0:1, :] = jnp.sum(jnp.where(keep, power, 0), axis=0, keepdims=True)
        right = jnp.zeros((PAIRS, LANES), i32)
        bz = right
        for b, (ox, oy, oz) in enumerate(SHELL):
            if (ox, oy) == (-cx, -cy):
                same = block == b
                bit = lax.shift_right_logical(occupied((0, 0), oz), part) & 1
                within = (lane + oz >= 2) & (lane + oz < CELLS + 2)
                right = jnp.where(same & within, bit, right)
                bz = jnp.where(same, oz, bz)
        keep = there & (right == 1) & (first != second)
        fx, fy, fz = face_of(first)
        columns = [(cx + a, cy + b) for a, b in ((0, 0), (1, 0), (-1, 0), (0, 1), (0, -1))]
        words[PAIRS * (g + 1) : PAIRS * (g + 2), :] = word_of(
            part, lane + bz - 2, first, lane + fz, cx + fx, cy + fy, fz - bz, columns
        )
        masks[1 + g : 2 + g, :] = jnp.sum(jnp.where(keep, power, 0), axis=0, keepdims=True)


def list_tasks(masks, words, spots, tasks):
    def row_step(row, n):
        for lane in range(1, CELLS + 3):
            spots[n] = row * LANES + lane
            n = n + (masks[row, lane] != 0).astype(i32)
        return n

    many = lax.fori_loop(0, 6, row_step, jnp.int32(0))

    def spot_step(s, n):
        spot = spots[s]
        row = lax.shift_right_logical(spot, 7)
        lane = spot & (LANES - 1)
        mask = masks[row, lane]
        for p in range(PAIRS):
            tasks[n] = words[PAIRS * row + p, lane]
            n = n + (lax.shift_right_logical(mask, p) & 1)
        return n

    return lax.fori_loop(0, many, spot_step, jnp.int32(0))


def extend(dest, pool, vel, ext, heads):
    x, y, z = place()
    heads[0:8, :] = jnp.zeros((8, LANES), i32)
    spots = ((-1, 0), (1, 0), (0, -1), (0, 1), (0, 0))
    for n, (dx, dy) in enumerate(spots):
        heads[n : n + 1, :] = heading_row(dest, x, y, dx, dy)
    turned = pltpu.roll(heads[0:8, :], z_shift(z), 1)
    heads[0:8, :] = turned
    heads[5:6, :] = pltpu.roll(turned, LANES - 1, 1)[4:5, :]
    heads[4:5, :] = pltpu.roll(turned, 1, 1)[4:5, :]
    valid = (heads[0:8, :] == iota((8, LANES), 0)).astype(f32)
    full = to_column(valid)
    turned = to_column(pool[P_B + AT_T : P_B + AT_T + 8, :])[2 * SEG + 2 : 2 * SEG + 2 + CELLS, :]
    ids = jnp.broadcast_to(turned[:, ROW_MIG : ROW_MIG + 1], (CELLS, LANES))
    many = jnp.broadcast_to(turned[:, ROW_COUNT : ROW_COUNT + 1], (CELLS, LANES))
    for s in range(2):
        keep = (many > float(s)) & (ids != float(s))
        for r in range(7):
            if r < 3:
                value = pool[pl.ds(P_B + r, CELLS, stride=4), :]
            elif r == 6:
                value = pool[pl.ds(P_B + 3, CELLS, stride=4), :]
            else:
                value = vel[pl.ds(2 * (r - 3) + s, CELLS, stride=6), :]
            ext[pl.ds(8 * r + s, CELLS, stride=56), :] = jnp.where(keep, value, 0.0)
    bundles = (P_XM, P_XP, P_BM, P_BP, P_B, P_B)
    for f in range(6):
        flag = jnp.broadcast_to(full[2 : 2 + CELLS, f : f + 1], (CELLS, LANES))
        for r in range(7):
            shift = float(FACES[f][r]) if r < 3 else 0.0
            if 3 <= r < 6:
                at, step = bundles[f] + AT_V + r - 3, 3
            else:
                at, step = bundles[f] + AT_O + min(r, 3), 4
            inner = CELLS - 1
            if f < 4:
                value = (pool[pl.ds(at, CELLS, stride=step), :] + shift) * flag
                ext[pl.ds(8 * r + 2 + f, CELLS, stride=56), :] = value
            elif f == 4:
                value = (pool[pl.ds(at, inner, stride=step), :] + shift) * flag[1:CELLS, :]
                ext[pl.ds(56 + 8 * r + 6, inner, stride=56), :] = value
                ext[8 * r + 6 : 8 * r + 7, :] = jnp.zeros((1, LANES), f32)
            else:
                value = (pool[pl.ds(at + step, inner, stride=step), :] + shift) * flag[0:inner, :]
                ext[pl.ds(8 * r + 7, inner, stride=56), :] = value
                last = 56 * inner + 8 * r + 7
                ext[last : last + 1, :] = jnp.zeros((1, LANES), f32)


def patch(dest, zlo, zhi, ext):
    x, y, z = place()
    rows = jnp.broadcast_to(heading_row(dest, x, y, 0, 0), (8, LANES))
    rows = pltpu.roll(rows, z_shift(z), 1)[0:1, :]
    thin = iota((1, LANES), 1)
    up = jnp.sum(jnp.where((thin == 1) & (rows == 4), 1.0, 0.0), axis=1, keepdims=True)
    down = jnp.sum(jnp.where((thin == CELLS + 2) & (rows == 5), 1.0, 0.0), axis=1, keepdims=True)
    for ref, flag, cell, slot, at, speed_at, shift in (
        (zlo, up, 0, 6, EDGE_AT[0, 0] + 12, E_V + 5, -1.0),
        (zhi, down, CELLS - 1, 7, EDGE_AT[0, 0] + 8, E_V, 1.0),
    ):
        for r in range(7):
            row = speed_at + r - 3 if 3 <= r < 6 else at + min(r, 3)
            value = (ref[row : row + 1, :] + (shift if r == 2 else 0.0)) * flag
            to = 56 * cell + 8 * r + slot
            ext[to : to + 1, :] = value


def add_forces(tasks, many, pool, edges, ext, forces):
    def spread(entry, a):
        if edges is None:
            row = pool[pl.ds(4 * entry + a, 1), :]
        else:
            near = pool[pl.ds(4 * jnp.minimum(entry, POOL // 4 - 1) + a, 1), :]
            which = jnp.maximum(entry - POOL // 4, 0)
            zlo, zhi = edges
            below = zlo[pl.ds(4 * jnp.minimum(which, EDGE // 4 - 1) + a, 1), :]
            above = zhi[pl.ds(4 * jnp.maximum(which - EDGE // 4, 0) + a, 1), :]
            row = jnp.where(entry < POOL // 4, near, jnp.where(which < EDGE // 4, below, above))
        wide = jnp.broadcast_to(row, (8, LANES))
        return pltpu.roll(wide, 0, 1, stride=1, stride_axis=0)

    def step(t, _):
        code = tasks[t]
        entry = code & 2047
        target = lax.shift_right_logical(code, 11) & 255
        base = lax.shift_right_logical(target, 3) * 56 + (target & 7)
        away = lax.shift_right_logical(code, 19)
        sx, sy, sz, ss = (spread(entry, a) for a in range(4))
        ts = ext[pl.ds(base + 48, 1), :]
        goal = []
        for a in range(3):
            shift = ((lax.shift_right_logical(away, 3 * a) & 7) - 2).astype(f32)
            wide = jnp.broadcast_to(ext[pl.ds(base + 8 * a, 1), :], (8, LANES))
            goal.append(wide - shift)
        tx, ty, tz = goal
        fx = jnp.zeros((8, LANES), f32)
        fy, fz = fx, fx
        for j in range(LANES // 8):
            dx = tx - (pltpu.roll(sx, 8 * j, 1) if j else sx)
            dy = ty - (pltpu.roll(sy, 8 * j, 1) if j else sy)
            dz = tz - (pltpu.roll(sz, 8 * j, 1) if j else sz)
            strong = pltpu.roll(ss, 8 * j, 1) if j else ss
            dist = dx * dx + dy * dy + dz * dz
            reach = jnp.maximum(1.0 - dist, 0.0)
            weight = strong * reach * reach / (dist + SOFTEN)
            fx = fx + weight * dx
            fy = fy + weight * dy
            fz = fz + weight * dz
        to = lax.shift_right_logical(target, 3) * 24 + (target & 7)
        for a, part in enumerate((fx, fy, fz)):
            total = jnp.sum(part, axis=0, keepdims=True) * ts
            forces[pl.ds(to + 8 * a, 1), :] += total
        return 0

    lax.fori_loop(0, many, step, 0)


def to_scalars(masks, words, masks_s, words_s, sems):
    one = pltpu.make_async_copy(masks, masks_s, sems.at[0])
    two = pltpu.make_async_copy(words, words_s, sems.at[1])
    one.start()
    two.start()
    return one, two


def early_kernel(
    dest, vel, pool, ext, forces, masks, words, heads, occ, turn, masks_s, words_s, spots, tasks, sems
):
    find_tasks(dest, pool, None, masks, words, heads, occ, turn)
    copies = to_scalars(masks, words, masks_s, words_s, sems)
    extend(dest, pool, vel, ext, heads)
    forces[...] = jnp.zeros_like(forces)
    for copy in copies:
        copy.wait()
    many = list_tasks(masks_s, words_s, spots, tasks)
    add_forces(tasks, many, pool, None, ext, forces)


def late_kernel(
    dest, pool, zlo, zhi, ext_in, forces_in, done, moved, forces,
    ext, total, masks, words, heads, occ, turn, masks_s, words_s, spots, tasks, sems,
):
    find_tasks(dest, pool, (zlo, zhi), masks, words, heads, occ, turn)
    masks[...] = masks[...] & ~done[...]
    copies = to_scalars(masks, words, masks_s, words_s, sems)
    ext[...] = ext_in[...]
    total[...] = forces_in[...]
    patch(dest, zlo, zhi, ext)
    for copy in copies:
        copy.wait()
    many = list_tasks(masks_s, words_s, spots, tasks)
    add_forces(tasks, many, pool, (zlo, zhi), ext, total)

    def finish(cell, _):
        for a in range(3):
            force = total[pl.ds(pl.multiple_of(24 * cell + 8 * a, 8), 8), :]
            forces[0, 0, cell, a] = force
            speed = ext[pl.ds(pl.multiple_of(56 * cell + 24 + 8 * a, 8), 8), :] + STEP * force
            moved[0, 0, cell, 3 + a] = speed
            moved[0, 0, cell, a] = (
                ext[pl.ds(pl.multiple_of(56 * cell + 8 * a, 8), 8), :] + STEP * speed
            )
        return 0

    lax.fori_loop(0, CELLS, finish, 0)


def whole(space=VMEM):
    return pl.BlockSpec(memory_space=space)


def rows_of(n, dtype=f32):
    return jax.ShapeDtypeStruct((n, LANES), dtype)


def limit(mib):
    return pltpu.CompilerParams(vmem_limit_bytes=mib * 2**20)


LIST_SCRATCH = [
    VMEM((6 * PAIRS, LANES), i32),
    VMEM((32, LANES), i32),
    VMEM((16, LANES), i32),
    VMEM((32, LANES), i32),
    SMEM((8, LANES), i32),
    SMEM((6 * PAIRS, LANES), i32),
    SMEM((6 * LANES + 16,), i32),
    SMEM((MAX_TASKS + 16,), i32),
    pltpu.SemaphoreType.DMA((2,)),
]


def per_device(
    positions,
    velocities,
    strength,
    cluster_count,
    migrant_ids,
    destination,
    pair_i,
    pair_j,
    pair_count,
):
    pos = positions.reshape((CELLS * 6, ATOMS))
    vel = velocities.reshape((CELLS * 6, ATOMS))
    stren = strength.reshape((CELLS * 2, ATOMS))
    dest = destination.reshape((NX * NY, LANES))
    B, O = pl.pallas_call(
        pack_kernel,
        out_shape=[rows_of(BUNDLE), rows_of(128)],
        in_specs=[whole()] * 8,
        out_specs=[whole()] * 2,
        compiler_params=limit(8),
        name="pack",
    )(
        pos, stren, vel, pair_i[0, 0].T, pair_j[0, 0].T,
        pair_count.reshape((1, CELLS)), migrant_ids.reshape((1, CELLS)), cluster_count.reshape((1, CELLS)),
    )
    cat = jnp.concatenate
    B_p, B_m, O_2 = moved_by(B, "gy", -1), moved_by(B, "gy", 1), moved_by(O, "gy", 2)
    near = cat([B, B_p[:SHORT], B_m[:SHORT], O_2], axis=0)
    far = cat([O, B_p[AT_O:AT_T], B_m[AT_O:AT_T]], axis=0)
    X_p, X_m = moved_by(near, "gx", -1), moved_by(near, "gx", 1)
    X2_p, X2_m = moved_by(far, "gx", -2), moved_by(far, "gx", 2)
    buffers = (B, B_p, B_m, O_2, X_p, X_m, X2_p, X2_m)
    low, high = pl.pallas_call(
        edges_kernel,
        out_shape=[rows_of(EDGE), rows_of(EDGE)],
        in_specs=[whole()] * 8,
        out_specs=[whole()] * 2,
        compiler_params=limit(8),
        name="edges",
    )(*buffers)
    zlo, zhi = moved_by(high, "gz", 1), moved_by(low, "gz", -1)
    pool = cat(buffers, axis=0)
    ext, early, done = pl.pallas_call(
        early_kernel,
        out_shape=[rows_of(CELLS * 56), rows_of(CELLS * 24), rows_of(8, i32)],
        in_specs=[whole()] * 3,
        out_specs=[whole()] * 3,
        scratch_shapes=LIST_SCRATCH,
        compiler_params=limit(16),
        name="early",
    )(dest, vel, pool)
    return pl.pallas_call(
        late_kernel,
        out_shape=[
            jax.ShapeDtypeStruct((1, 1, CELLS, 6, 8, LANES), f32),
            jax.ShapeDtypeStruct((1, 1, CELLS, 3, 8, LANES), f32),
        ],
        in_specs=[whole()] * 7,
        out_specs=[whole()] * 2,
        scratch_shapes=[VMEM((CELLS * 56, LANES), f32), VMEM((CELLS * 24, LANES), f32), VMEM((8, LANES), i32)]
        + LIST_SCRATCH,
        compiler_params=limit(16),
        name="late",
    )(dest, pool, zlo, zhi, ext, early, done)


def solution(mesh):
    in_specs = (
        P("gx", "gy", "gz", None, None, None),
        P("gx", "gy", "gz", None, None, None),
        P("gx", "gy", "gz", None, None),
        P("gx", "gy", "gz"),
        P("gx", "gy", "gz", None),
        P(),
        P("gx", "gy", "gz", None),
        P("gx", "gy", "gz", None),
        P("gx", "gy", "gz"),
    )
    out_specs = (P("gx", "gy", "gz", None, None, None), P("gx", "gy", "gz", None, None, None))
    return jax.shard_map(
        per_device, mesh=mesh, in_specs=in_specs, out_specs=out_specs, check_vma=False
    )
```

```python
import numpy as np
import jax
import jax.numpy as jnp
from jax import lax
from jax.experimental import pallas as pl
from jax.experimental.pallas import tpu as pltpu
from jax.sharding import PartitionSpec as P

FACES = ((-1, 0, 0), (1, 0, 0), (0, -1, 0), (0, 1, 0), (0, 0, -1), (0, 0, 1))
SHELL = (
    (0, 0, 0),
    (0, 0, 1),
    (0, 1, -1),
    (0, 1, 0),
    (0, 1, 1),
    (1, -1, -1),
    (1, -1, 0),
    (1, -1, 1),
    (1, 0, -1),
    (1, 0, 0),
    (1, 0, 1),
    (1, 1, -1),
    (1, 1, 0),
    (1, 1, 1),
)
STEP = 0.01
EARLY_UNROLL, LATE_UNROLL = 8, 4
SOFTEN = 0.1
CELLS = 32
WIDE = CELLS + 4
ATOMS = 128
PAIRS = 16
NX, NY = 16, 4
LANES = 128
SEG = 40
ROW_LIVE, ROW_MIG, ROW_COUNT = 0, 1, 2
BEHIND = ((0, 0), (0, -1), (-1, 1), (-1, 0), (-1, -1))
NEAR = tuple((dx, dy) for dx in (-1, 0, 1) for dy in (-1, 0, 1))
MAX_TASKS = CELLS * PAIRS + len(BEHIND) * (CELLS + 2) * PAIRS

SMEM = pltpu.SMEM
VMEM = pltpu.VMEM
f32 = jnp.float32
bf16 = jnp.bfloat16
i32 = jnp.int32

OUT_T, AT_S, AT_V, BUNDLE = 128, 144, 272, 368
X1 = BUNDLE + 2 * AT_V + 128
X2 = 384
SIZES = (BUNDLE, BUNDLE, BUNDLE, 128, X1, X1, X2, X2)
P_B, P_OP, P_OM, P_O2, P_XP, P_XM, P_X2P, P_X2M, POOL = (sum(SIZES[:n]) for n in range(len(SIZES) + 1))


def column_rows():
    out = {(0, 0): P_B, (0, 1): P_OP, (0, -1): P_OM}
    for dx, x1, x2 in ((1, P_XP, P_X2P), (-1, P_XM, P_X2M)):
        out[dx, 0], out[dx, 1], out[dx, -1] = x1, x1 + BUNDLE, x1 + BUNDLE + AT_V
        for n, dy in enumerate((0, 1, -1)):
            out[2 * dx, dy] = x2 + n * 128
    stay = {c: at + AT_S for c, at in out.items() if abs(c[0]) < 2}
    for dy in (-2, 2):
        out[0, dy] = P_O2
        for dx, x1 in ((1, P_XP), (-1, P_XM)):
            out[dx, dy] = x1 + BUNDLE + 2 * AT_V
    return out, stay


OUT_AT, STAY_AT = column_rows()
FAR = tuple(c for c in ((0, 2), (1, 2), (-1, 2), (2, 0), (2, 1), (2, -1), (-2, 0), (-2, 1), (-2, -1)))
E_T = 16 * len(NEAR) + 8 * len(FAR)
E_V = E_T + 16
EDGE = E_V + 8
EDGE_AT = {c: 16 * n for n, c in enumerate(NEAR)}
for _n, _c in enumerate(FAR):
    EDGE_AT[_c] = 16 * len(NEAR) + 8 * _n - 8
    if _c[1] == 2:
        EDGE_AT[_c[0], -2] = EDGE_AT[_c]


def moved_by(array, axis, by):
    size = lax.axis_size(axis)
    return lax.ppermute(array, axis, [(i, (i + by) % size) for i in range(size)])


def to_column(rows):
    pad = jnp.zeros((LANES - rows.shape[0], LANES), f32)
    return jnp.concatenate([rows, pad], axis=0).T


def pack_kernel(*refs):
    sources, (bundle, alone), held, sems = refs[:8], refs[8:10], refs[10:18], refs[18]
    copies = [pltpu.make_async_copy(a, b, sems.at[n]) for n, (a, b) in enumerate(zip(sources, held))]
    for copy in copies:
        copy.start()
    for copy in copies:
        copy.wait()
    pos, stren, vel, first, second, live, mig, count = held
    bundle[OUT_T : OUT_T + 16, :] = jnp.zeros((16, LANES), f32)
    bundle[OUT_T : OUT_T + 16, 2 : 2 + CELLS] = first[...].astype(f32)
    bundle[OUT_T : OUT_T + 16, SEG + 2 : SEG + 2 + CELLS] = second[...].astype(f32)
    low = 2 * SEG + 2
    for row, ref in ((ROW_LIVE, live), (ROW_MIG, mig), (ROW_COUNT, count)):
        bundle[OUT_T + row : OUT_T + row + 1, low : low + CELLS] = ref[...].astype(f32)
    turned = to_column(bundle[OUT_T : OUT_T + 8, :])[low : low + CELLS, :]
    ids = jnp.broadcast_to(turned[:, ROW_MIG : ROW_MIG + 1], (CELLS, LANES))
    many = jnp.broadcast_to(turned[:, ROW_COUNT : ROW_COUNT + 1], (CELLS, LANES))
    low_slot = ids == 0.0
    kept = (1.0 - ids) < many
    filled = ids < many
    for c in range(4):
        if c < 3:
            one = pos[pl.ds(2 * c, CELLS, stride=6), :]
            two = pos[pl.ds(2 * c + 1, CELLS, stride=6), :]
        else:
            one = stren[pl.ds(0, CELLS, stride=2), :]
            two = stren[pl.ds(1, CELLS, stride=2), :]
        stay = jnp.where(kept, jnp.where(low_slot, two, one), 0.0)
        out = jnp.where(filled, jnp.where(low_slot, one, two), 0.0)
        bundle[pl.ds(AT_S + c, CELLS, stride=4), :] = stay
        bundle[pl.ds(c, CELLS, stride=4), :] = out
        alone[pl.ds(c, CELLS, stride=4), :] = out
    for c in range(3):
        one = vel[pl.ds(2 * c, CELLS, stride=6), :]
        two = vel[pl.ds(2 * c + 1, CELLS, stride=6), :]
        speed = jnp.where(filled, jnp.where(low_slot, one, two), 0.0)
        bundle[pl.ds(AT_V + c, CELLS, stride=3), :] = speed


def place():
    return lax.axis_index("gx"), lax.axis_index("gy"), lax.axis_index("gz")


def heading_row(dest, x, y, dx, dy):
    row = lax.rem(x + (dx + NX), NX) * NY + lax.rem(y + (dy + NY), NY)
    return dest[pl.ds(row, 1), :]


def z_shift(z):
    return lax.rem(LANES + 2 - z * CELLS, LANES)


def iota(shape, axis):
    return lax.broadcasted_iota(i32, shape, axis)


def edges_kernel(b, op, om, o2, xp, xm, x2p, x2m, low, high):
    parts = (
        (P_B, b), (P_OP, op), (P_OM, om), (P_O2, o2),
        (P_XP, xp), (P_XM, xm), (P_X2P, x2p), (P_X2M, x2m),
    )

    def find(row):
        for start, ref in reversed(parts):
            if row >= start:
                return ref, row - start

    lane = iota((16, LANES), 1)
    for side, ref, cell in ((0, low, 0), (1, high, CELLS - 2)):
        table = jnp.zeros((16, LANES), f32)
        for n, column in enumerate(NEAR):
            source, row = find(OUT_AT[column])
            to = EDGE_AT[column]
            first = row + AT_S + 4 * cell
            ref[to : to + 8, :] = source[first : first + 8, :]
            ref[to + 8 : to + 16, :] = source[row + 4 * cell : row + 4 * cell + 8, :]
            values = source[row + OUT_T : row + OUT_T + 16, :]
            rolled = pltpu.roll(values, (2 * n - 2 - cell) % LANES, 1)
            for s in range(3):
                here = (lane >= s * SEG + 2 * n) & (lane < s * SEG + 2 * n + 2)
                table = jnp.where(here, rolled, table)
        for column in FAR:
            source, row = find(OUT_AT[column])
            to = EDGE_AT[column] + 8
            ref[to : to + 8, :] = source[row + 4 * cell : row + 4 * cell + 8, :]
        ref[E_T : E_T + 16, :] = table
        at = AT_V + (88 if side else 0)
        ref[E_V : E_V + 8, :] = b[at : at + 8, :]


def find_tasks(dest, near_tables, edges, masks, words, heads, occ, turn):
    x, y, z = place()
    heads[...] = jnp.zeros_like(heads)
    for dx in range(-2, 3):
        for dy in range(-2, 3):
            if abs(dx) + abs(dy) < 4:
                at = (dx + 2) * 5 + dy + 2
                heads[at : at + 1, :] = heading_row(dest, x, y, dx, dy)
    heads[...] = pltpu.roll(heads[...], z_shift(z), 1)

    def head(dx, dy):
        at = (dx + 2) * 5 + dy + 2
        return heads[at : at + 1, :]

    slot = iota((PAIRS, LANES), 0)
    lane = iota((PAIRS, LANES), 1)
    thin = iota((1, LANES), 1)
    tables = {}
    for n, column in enumerate(NEAR):
        ref, row = near_tables[column]
        values = ref[row : row + 16, :]
        if edges is not None:
            zlo, zhi = edges
            below = pltpu.roll(zlo[E_T : E_T + 16, :], (-2 * n) % LANES, 1)
            above = pltpu.roll(zhi[E_T : E_T + 16, :], (34 - 2 * n) % LANES, 1)
            for s in range(3):
                values = jnp.where((lane >= s * SEG) & (lane < s * SEG + 2), below, values)
                values = jnp.where((lane >= s * SEG + 34) & (lane < s * SEG + 36), above, values)
        tables[column] = values.astype(i32)
    rest = {c: pltpu.roll(tables[c], LANES - 2 * SEG, 1) for c in NEAR}
    ids = {c: rest[c][ROW_MIG : ROW_MIG + 1, :] for c in NEAR}
    counts = {c: rest[c][ROW_COUNT : ROW_COUNT + 1, :] for c in NEAR}
    filled = {c: (ids[c] < counts[c]).astype(i32) for c in NEAR}
    if edges is None:
        default = ((thin >= 2) & (thin < CELLS + 2)).astype(i32)
    else:
        default = jnp.ones((1, LANES), i32)

    def coming(dx, dy, face):
        return (head(dx, dy) == face).astype(i32) * filled.get((dx, dy), default)

    occ[...] = jnp.zeros_like(occ)
    turn[...] = jnp.zeros_like(turn)
    for n, (dx, dy) in enumerate(NEAR):
        turn[n : n + 1, :] = coming(dx, dy, 4) * 64
        turn[16 + n : 17 + n, :] = coming(dx, dy, 5) * 128
    from_below = pltpu.roll(turn[0:16, :], 1, 1)
    from_above = pltpu.roll(turn[16:32, :], LANES - 1, 1)
    for n, (dx, dy) in enumerate(NEAR):
        c = (dx, dy)
        kept0 = ((counts[c] > 0) & (ids[c] != 0)).astype(i32)
        kept1 = ((counts[c] > 1) & (ids[c] != 1)).astype(i32)
        sides = (
            coming(dx - 1, dy, 0) * 4
            + coming(dx + 1, dy, 1) * 8
            + coming(dx, dy - 1, 2) * 16
            + coming(dx, dy + 1, 3) * 32
        )
        occ[n : n + 1, :] = kept0 + 2 * kept1 + sides
    here = occ[...] + from_below + from_above
    by_z = {0: here, 1: pltpu.roll(here, LANES - 1, 1), -1: pltpu.roll(here, 1, 1)}

    def occupied(column, dz):
        n = NEAR.index(column)
        return jnp.broadcast_to(by_z[dz][n : n + 1, :], (PAIRS, LANES))

    def face_of(k):
        fx = jnp.where(k == 3, 1, jnp.where(k == 2, -1, 0))
        fy = jnp.where(k == 5, 1, jnp.where(k == 4, -1, 0))
        fz = jnp.where(k == 7, 1, jnp.where(k == 6, -1, 0))
        return fx, fy, fz

    def word_of(mine, target, theirs, at, vx, vy, vz, columns):
        half = (theirs >= 2).astype(i32)
        which = (vx + 2) * 5 + vy + 2
        inner = jnp.zeros_like(slot)
        outer = jnp.zeros_like(slot)
        stays = jnp.zeros_like(slot)
        for cx, cy in columns:
            same = which == (cx + 2) * 5 + cy + 2
            inner = jnp.where(same, OUT_AT[cx, cy] // 4, inner)
            if (cx, cy) in STAY_AT:
                stays = jnp.where(same, STAY_AT[cx, cy] // 4, stays)
            if edges is not None:
                outer = jnp.where(same, EDGE_AT[cx, cy] // 4, outer)
        entry = jnp.where(half == 1, inner, stays) + at - 2
        if edges is not None:
            low_edge = outer + 2 * half + at + POOL // 4
            high_edge = outer + 2 * half + at - 34 + (POOL + EDGE) // 4
            entry = jnp.where(at < 2, low_edge, jnp.where(at >= CELLS + 2, high_edge, entry))
        return (
            entry
            + (target * 8 + mine) * 2048
            + ((vx + 2) + 8 * (vy + 2) + 64 * (vz + 2)) * (2048 * 256)
        )

    masks[...] = jnp.zeros_like(masks)
    power = lax.shift_left(jnp.ones_like(slot), slot)
    for g, column in enumerate(BEHIND):
        cx, cy = column
        inside = lane < WIDE
        first = jnp.where(inside, tables[column], 0)
        second = jnp.where(inside, pltpu.roll(tables[column], LANES - SEG, 1), 0)
        live = inside & (slot < rest[column][ROW_LIVE : ROW_LIVE + 1, :])
        block = lax.shift_right_logical(second, 3)
        part = second & 7
        there = live & ((lax.shift_right_logical(occupied(column, 0), first) & 1) == 1)
        if g == 0:
            left = jnp.zeros((PAIRS, LANES), i32)
            bx, by, bz = left, left, left
            for b, (ox, oy, oz) in enumerate(SHELL):
                same = block == b
                bit = lax.shift_right_logical(occupied((ox, oy), oz), part) & 1
                left = jnp.where(same, bit, left)
                bx = jnp.where(same, ox, bx)
                by = jnp.where(same, oy, by)
                bz = jnp.where(same, oz, bz)
            keep = there & (left == 1) & (lane >= 2) & (lane < CELLS + 2)
            fx, fy, fz = face_of(part)
            found = [word_of(
                first, lane - 2, part, lane + bz + fz, bx + fx, by + fy, bz + fz, OUT_AT
            )]
            masks[0:1, :] = jnp.sum(jnp.where(keep, power, 0), axis=0, keepdims=True)
        right = jnp.zeros((PAIRS, LANES), i32)
        bz = right
        for b, (ox, oy, oz) in enumerate(SHELL):
            if (ox, oy) == (-cx, -cy):
                same = block == b
                bit = lax.shift_right_logical(occupied((0, 0), oz), part) & 1
                within = (lane + oz >= 2) & (lane + oz < CELLS + 2)
                right = jnp.where(same & within, bit, right)
                bz = jnp.where(same, oz, bz)
        keep = there & (right == 1) & (first != second)
        fx, fy, fz = face_of(first)
        columns = [(cx + a, cy + b) for a, b in ((0, 0), (1, 0), (-1, 0), (0, 1), (0, -1))]
        found.append(
            word_of(part, lane + bz - 2, first, lane + fz, cx + fx, cy + fy, fz - bz, columns)
        )
        masks[1 + g : 2 + g, :] = jnp.sum(jnp.where(keep, power, 0), axis=0, keepdims=True)
    masks[7:8, :] = jnp.sum(masks[0:6, :], axis=0, keepdims=True)
    for n in range(2):
        one, two, three = found[3 * n : 3 * n + 3]
        two, three = pltpu.roll(two, SEG, 1), pltpu.roll(three, 2 * SEG, 1)
        packed = jnp.where(lane < SEG, one, jnp.where(lane < 2 * SEG, two, three))
        words[PAIRS * n : PAIRS * (n + 1), :] = packed


def lowest_bit(mask):
    low = mask & -mask
    at = jnp.int32(0)
    for step, bits in ((8, 0xFF00), (4, 0xF0F0), (2, 0xCCCC), (1, 0xAAAA)):
        at = at + jnp.where((low & bits) != 0, step, 0)
    return at


def list_tasks(masks, words, spots, tasks, ready):
    many = jnp.int32(0)
    for lane in range(1, CELLS + 3):
        spots[many] = lane
        many = many + (masks[7, lane] != 0).astype(i32)

    def lane_step(s, n):
        lane = spots[s]
        for row in range(6):
            mask = masks[row, lane]
            spots[LANES + n] = mask
            spots[8 * LANES + n] = row // 3 * PAIRS * LANES + row % 3 * SEG + lane
            n = n + (mask != 0).astype(i32)
        return n

    found = lax.fori_loop(0, many, lane_step, jnp.int32(0))
    ready()

    def spot_step(s, n):
        spot = spots[8 * LANES + s]
        row = lax.shift_right_logical(spot, 7)
        lane = spot & (LANES - 1)

        def left(state):
            return state[0] != 0

        def take(state):
            mask, n = state
            tasks[n] = words[row + lowest_bit(mask), lane]
            return mask & (mask - 1), n + 1

        return lax.while_loop(left, take, take((spots[LANES + s], n)))[1]

    n = lax.fori_loop(0, found, spot_step, jnp.int32(0))
    for u in range(EARLY_UNROLL - 1):
        tasks[n + u] = 0
    return n


def extend(dest, pool, vel, ext, heads):
    x, y, z = place()
    heads[0:8, :] = jnp.zeros((8, LANES), i32)
    spots = ((-1, 0), (1, 0), (0, -1), (0, 1), (0, 0))
    for n, (dx, dy) in enumerate(spots):
        heads[n : n + 1, :] = heading_row(dest, x, y, dx, dy)
    turned = pltpu.roll(heads[0:8, :], z_shift(z), 1)
    heads[0:8, :] = turned
    heads[5:6, :] = pltpu.roll(turned, LANES - 1, 1)[4:5, :]
    heads[4:5, :] = pltpu.roll(turned, 1, 1)[4:5, :]
    valid = (heads[0:8, :] == iota((8, LANES), 0)).astype(f32)
    full = to_column(valid)
    turned = to_column(pool[P_B + OUT_T : P_B + OUT_T + 8, :])
    turned = turned[2 * SEG + 2 : 2 * SEG + 2 + CELLS, :]
    ids = jnp.broadcast_to(turned[:, ROW_MIG : ROW_MIG + 1], (CELLS, LANES))
    many = jnp.broadcast_to(turned[:, ROW_COUNT : ROW_COUNT + 1], (CELLS, LANES))
    for s in range(2):
        keep = (many > float(s)) & (ids != float(s))
        for r in range(7):
            if r < 3:
                value = pool[pl.ds(P_B + AT_S + r, CELLS, stride=4), :]
            elif r == 6:
                value = pool[pl.ds(P_B + AT_S + 3, CELLS, stride=4), :]
            else:
                value = vel[pl.ds(2 * (r - 3) + s, CELLS, stride=6), :]
            ext[pl.ds(8 * r + s, CELLS, stride=56), :] = jnp.where(keep, value, 0.0)
    places = (P_XM, P_XP, P_OM, P_OP, P_B, P_B)
    for f in range(6):
        flag = jnp.broadcast_to(full[2 : 2 + CELLS, f : f + 1], (CELLS, LANES))
        for r in range(7):
            shift = float(FACES[f][r]) if r < 3 else 0.0
            if 3 <= r < 6:
                at, step = places[f] + AT_V + r - 3, 3
            else:
                at, step = places[f] + min(r, 3), 4
            inner = CELLS - 1
            if f < 4:
                value = (pool[pl.ds(at, CELLS, stride=step), :] + shift) * flag
                ext[pl.ds(8 * r + 2 + f, CELLS, stride=56), :] = value
            elif f == 4:
                value = (pool[pl.ds(at, inner, stride=step), :] + shift) * flag[1:CELLS, :]
                ext[pl.ds(56 + 8 * r + 6, inner, stride=56), :] = value
                ext[8 * r + 6 : 8 * r + 7, :] = jnp.zeros((1, LANES), f32)
            else:
                value = (pool[pl.ds(at + step, inner, stride=step), :] + shift) * flag[0:inner, :]
                ext[pl.ds(8 * r + 7, inner, stride=56), :] = value
                last = 56 * inner + 8 * r + 7
                ext[last : last + 1, :] = jnp.zeros((1, LANES), f32)


def patch(dest, zlo, zhi, ext):
    x, y, z = place()
    rows = jnp.broadcast_to(heading_row(dest, x, y, 0, 0), (8, LANES))
    rows = pltpu.roll(rows, z_shift(z), 1)[0:1, :]
    thin = iota((1, LANES), 1)
    up = jnp.sum(jnp.where((thin == 1) & (rows == 4), 1.0, 0.0), axis=1, keepdims=True)
    down = jnp.sum(jnp.where((thin == CELLS + 2) & (rows == 5), 1.0, 0.0), axis=1, keepdims=True)
    for ref, flag, cell, slot, at, speed_at, shift in (
        (zlo, up, 0, 6, EDGE_AT[0, 0] + 12, E_V + 5, -1.0),
        (zhi, down, CELLS - 1, 7, EDGE_AT[0, 0] + 8, E_V, 1.0),
    ):
        for r in range(7):
            row = speed_at + r - 3 if 3 <= r < 6 else at + min(r, 3)
            value = (ref[row : row + 1, :] + (shift if r == 2 else 0.0)) * flag
            to = 56 * cell + 8 * r + slot
            ext[to : to + 1, :] = value


def inverse(value):
    return pl.reciprocal(value, approx=True)


def split(value):
    one = value.astype(bf16).astype(f32)
    rest = value - one
    two = rest.astype(bf16).astype(f32)
    return one, two, rest - two


def add_forces(tasks, many, pool, edges, ext, forces):
    unroll = EARLY_UNROLL if edges is None else LATE_UNROLL
    row = iota((8, LANES), 0)
    top = row < 4
    last = (row & 3) == 3

    def source_of(entry):
        near = pool[pl.ds(4 * jnp.minimum(entry, POOL // 4 - 1), 4), :]
        if edges is not None:
            which = jnp.maximum(entry - POOL // 4, 0)
            zlo, zhi = edges
            below = zlo[pl.ds(4 * jnp.minimum(which, EDGE // 4 - 1), 4), :]
            above = zhi[pl.ds(4 * jnp.maximum(which - EDGE // 4, 0), 4), :]
            near = jnp.where(entry < POOL // 4, near, jnp.where(which < EDGE // 4, below, above))
        return jnp.concatenate([near, near], axis=0)

    def length(value):
        return jnp.sum(jnp.where(top & ~last, value * value, 0.0), axis=0, keepdims=True)

    def one(code, live):
        entry = code & 2047
        target = lax.shift_right_logical(code, 11) & 255
        base = lax.shift_right_logical(target, 3) * 56 + (target & 7)
        away = lax.shift_right_logical(code, 19)
        raw = source_of(entry)
        source = jnp.where(last, raw, raw - 0.5)
        goal = jnp.zeros((8, LANES), f32)
        for a in range(3):
            shift = ((lax.shift_right_logical(away, 3 * a) & 7) - 2).astype(f32)
            wide = jnp.broadcast_to(ext[pl.ds(base + 8 * a, 1), :], (8, LANES))
            goal = jnp.where((row & 3) == a, wide - shift - 0.5, goal)
        strong = ext[pl.ds(base + 48, 1), :] * live
        s1, s2, s3 = split(source)
        t1, t2, t3 = split(goal)
        a1, a2, a3 = split(jnp.broadcast_to(-length(source), (8, LANES)))
        b1, b2, b3 = split(jnp.broadcast_to(1.0 - length(goal), (8, LANES)))
        w1, w2, w3 = 2.0 * s1, 2.0 * s2, 2.0 * s3
        left = jnp.concatenate(
            [
                jnp.where(last, jnp.where(top, a1, a2), jnp.where(top, w1, w2)),
                jnp.where(last, 1.0, jnp.where(top, w1, w2)),
                jnp.where(last, jnp.where(top, a3, 1.0), jnp.where(top, w1, w3)),
                jnp.zeros((8, LANES), f32),
            ],
            axis=0,
        ).astype(bf16)
        right = jnp.concatenate(
            [
                jnp.where(last, 1.0, t1),
                jnp.where(last, jnp.where(top, b1, b2), t2),
                jnp.where(last, jnp.where(top, 1.0, b3), jnp.where(top, t3, t1)),
                jnp.zeros((8, LANES), f32),
            ],
            axis=0,
        ).astype(bf16)
        inside = lax.dot_general(left, right, (((0,), (0,)), ((), ())), preferred_element_type=f32)
        reach = jnp.maximum(inside, 0.0)
        weight = reach * reach * inverse((1.0 + SOFTEN) - reach)
        high = weight.astype(bf16)
        low = (weight - high.astype(f32)).astype(bf16)
        gain = jnp.broadcast_to(raw[3:4, :], (8, LANES))
        v1, v2, v3 = split(jnp.where(last, gain, gain * source))
        moment = jnp.concatenate([jnp.where(top, v1, v2), jnp.where(top, v3, 0.0)], axis=0).astype(bf16)
        sums = jnp.dot(
            jnp.concatenate([moment, moment], axis=1),
            jnp.concatenate([high, low], axis=0),
            preferred_element_type=f32,
        )
        sums = sums[0:8, :] + sums[8:16, :]
        sums = sums[0:4, :] + sums[4:8, :]
        push = (goal[0:4, :] * sums[3:4, :] - sums) * strong
        to = lax.shift_right_logical(target, 3) * 24 + (target & 7)
        return to, push

    def step(t, _):
        at = unroll * t
        results = [one(tasks[at + u], (at + u < many).astype(f32)) for u in range(unroll)]
        for to, push in results:
            for a in range(3):
                forces[pl.ds(to + 8 * a, 1), :] += push[a : a + 1, :]
        return 0

    lax.fori_loop(0, lax.div(many + (unroll - 1), unroll), step, 0)


def to_scalars(masks, words, masks_s, words_s, sems):
    one = pltpu.make_async_copy(masks, masks_s, sems.at[0])
    two = pltpu.make_async_copy(words, words_s, sems.at[1])
    one.start()
    two.start()
    return one, two


def flags_kernel(dest, b, op, om, xp, xm, masks, words, heads, occ, turn):
    parts = ((P_B, b), (P_OP, op), (P_OM, om), (P_XP, xp), (P_XM, xm))
    tables = {}
    for column in NEAR:
        row = OUT_AT[column] + OUT_T
        start, ref = [part for part in parts if part[0] <= row][-1]
        tables[column] = (ref, row - start)
    find_tasks(dest, tables, None, masks, words, heads, occ, turn)


def early_kernel(
    dest, vel, pool, masks, words, ext, forces, heads, masks_s, words_s, spots, tasks, sems
):
    copies = to_scalars(masks, words, masks_s, words_s, sems)
    extend(dest, pool, vel, ext, heads)
    forces[...] = jnp.zeros_like(forces)
    copies[0].wait()
    many = list_tasks(masks_s, words_s, spots, tasks, copies[1].wait)
    add_forces(tasks, many, pool, None, ext, forces)


def late_kernel(
    dest, pool, zlo, zhi, ext_in, forces_in, done, moved, forces,
    ext, total, masks, words, occ, turn, heads, masks_s, words_s, spots, tasks, sems,
):
    tables = {c: (pool, OUT_AT[c] + OUT_T) for c in NEAR}
    find_tasks(dest, tables, (zlo, zhi), masks, words, heads, occ, turn)
    rest = masks[0:6, :] & ~done[0:6, :]
    masks[0:6, :] = rest
    masks[7:8, :] = jnp.sum(rest, axis=0, keepdims=True)
    copies = to_scalars(masks, words, masks_s, words_s, sems)
    ext[...] = ext_in[...]
    total[...] = forces_in[...]
    patch(dest, zlo, zhi, ext)
    copies[0].wait()
    many = list_tasks(masks_s, words_s, spots, tasks, copies[1].wait)
    add_forces(tasks, many, pool, (zlo, zhi), ext, total)

    def finish(cell, _):
        for a in range(3):
            force = total[pl.ds(pl.multiple_of(24 * cell + 8 * a, 8), 8), :]
            forces[0, 0, cell, a] = force
            speed = ext[pl.ds(pl.multiple_of(56 * cell + 24 + 8 * a, 8), 8), :] + STEP * force
            moved[0, 0, cell, 3 + a] = speed
            moved[0, 0, cell, a] = (
                ext[pl.ds(pl.multiple_of(56 * cell + 8 * a, 8), 8), :] + STEP * speed
            )
        return 0

    lax.fori_loop(0, CELLS, finish, 0)


def whole(space=VMEM):
    return pl.BlockSpec(memory_space=space)


def rows_of(n, dtype=f32):
    return jax.ShapeDtypeStruct((n, LANES), dtype)


def limit(mib):
    return pltpu.CompilerParams(vmem_limit_bytes=mib * 2**20)


WORDS = 2 * PAIRS
FIND_SCRATCH = [VMEM((16, LANES), i32), VMEM((32, LANES), i32)]
LIST_SCRATCH = [
    VMEM((32, LANES), i32),
    SMEM((8, LANES), i32),
    SMEM((WORDS, LANES), i32),
    SMEM((16 * LANES,), i32),
    SMEM((MAX_TASKS + 16,), i32),
    pltpu.SemaphoreType.DMA((2,)),
]


def per_device(
    positions,
    velocities,
    strength,
    cluster_count,
    migrant_ids,
    destination,
    pair_i,
    pair_j,
    pair_count,
):
    pos = positions.reshape((CELLS * 6, ATOMS))
    vel = velocities.reshape((CELLS * 6, ATOMS))
    stren = strength.reshape((CELLS * 2, ATOMS))
    dest = destination.reshape((NX * NY, LANES))
    B, O = pl.pallas_call(
        pack_kernel,
        out_shape=[rows_of(BUNDLE), rows_of(128)],
        in_specs=[whole(pltpu.HBM)] * 8,
        out_specs=[whole()] * 2,
        scratch_shapes=[
            VMEM((CELLS * 6, ATOMS), f32),
            VMEM((CELLS * 2, ATOMS), f32),
            VMEM((CELLS * 6, ATOMS), f32),
            VMEM((PAIRS, CELLS), i32),
            VMEM((PAIRS, CELLS), i32),
            VMEM((1, CELLS), i32),
            VMEM((1, CELLS), i32),
            VMEM((1, CELLS), i32),
            pltpu.SemaphoreType.DMA((8,)),
        ],
        compiler_params=limit(8),
        name="pack",
    )(
        *(
            pltpu.with_memory_space_constraint(a, pltpu.HBM)
            for a in (
                pos, stren, vel, pair_i[0, 0].T, pair_j[0, 0].T,
                pair_count.reshape((1, CELLS)), migrant_ids.reshape((1, CELLS)), cluster_count.reshape((1, CELLS)),
            )
        )
    )
    cat = jnp.concatenate
    O_2 = moved_by(O, "gy", 2)
    B_p, B_m = moved_by(B, "gy", -1), moved_by(B, "gy", 1)
    near = cat([B, B_p[:AT_V], B_m[:AT_V], O_2], axis=0)
    far = cat([O, B_p[:128], B_m[:128]], axis=0)
    X_p, X_m = moved_by(near, "gx", -1), moved_by(near, "gx", 1)
    X2_p, X2_m = moved_by(far, "gx", -2), moved_by(far, "gx", 2)
    buffers = (B, B_p, B_m, O_2, X_p, X_m, X2_p, X2_m)
    low, high = pl.pallas_call(
        edges_kernel,
        out_shape=[rows_of(EDGE), rows_of(EDGE)],
        in_specs=[whole()] * 8,
        out_specs=[whole()] * 2,
        compiler_params=limit(8),
        name="edges",
    )(*buffers)
    zlo, zhi = moved_by(high, "gz", 1), moved_by(low, "gz", -1)
    masks, words = pl.pallas_call(
        flags_kernel,
        out_shape=[rows_of(8, i32), rows_of(WORDS, i32)],
        in_specs=[whole()] * 6,
        out_specs=[whole()] * 2,
        scratch_shapes=[VMEM((32, LANES), i32)] + FIND_SCRATCH,
        compiler_params=limit(8),
        name="flags",
    )(dest, B, B_p, B_m, X_p, X_m)
    pool = cat(buffers, axis=0)
    ext, early = pl.pallas_call(
        early_kernel,
        out_shape=[rows_of(CELLS * 56), rows_of(CELLS * 24)],
        in_specs=[whole()] * 5,
        out_specs=[whole()] * 2,
        scratch_shapes=LIST_SCRATCH,
        compiler_params=limit(16),
        name="early",
    )(dest, vel, pool, masks, words)
    return pl.pallas_call(
        late_kernel,
        out_shape=[
            jax.ShapeDtypeStruct((1, 1, CELLS, 6, 8, LANES), f32),
            jax.ShapeDtypeStruct((1, 1, CELLS, 3, 8, LANES), f32),
        ],
        in_specs=[whole()] * 7,
        out_specs=[whole()] * 2,
        scratch_shapes=[
            VMEM((CELLS * 56, LANES), f32),
            VMEM((CELLS * 24, LANES), f32),
            VMEM((8, LANES), i32),
            VMEM((WORDS, LANES), i32),
        ]
        + FIND_SCRATCH
        + LIST_SCRATCH,
        compiler_params=limit(16),
        name="late",
    )(dest, pool, zlo, zhi, ext, early, masks)


def solution(mesh):
    in_specs = (
        P("gx", "gy", "gz", None, None, None),
        P("gx", "gy", "gz", None, None, None),
        P("gx", "gy", "gz", None, None),
        P("gx", "gy", "gz"),
        P("gx", "gy", "gz", None),
        P(),
        P("gx", "gy", "gz", None),
        P("gx", "gy", "gz", None),
        P("gx", "gy", "gz"),
    )
    out_specs = (P("gx", "gy", "gz", None, None, None), P("gx", "gy", "gz", None, None, None))
    return jax.shard_map(
        per_device, mesh=mesh, in_specs=in_specs, out_specs=out_specs, check_vma=False
    )
```

```python
import numpy as np
import jax
import jax.numpy as jnp
from jax import lax
from jax.experimental import pallas as pl
from jax.experimental.pallas import tpu as pltpu
from jax.sharding import PartitionSpec as P

FACES = ((-1, 0, 0), (1, 0, 0), (0, -1, 0), (0, 1, 0), (0, 0, -1), (0, 0, 1))
SHELL = (
    (0, 0, 0),
    (0, 0, 1),
    (0, 1, -1),
    (0, 1, 0),
    (0, 1, 1),
    (1, -1, -1),
    (1, -1, 0),
    (1, -1, 1),
    (1, 0, -1),
    (1, 0, 0),
    (1, 0, 1),
    (1, 1, -1),
    (1, 1, 0),
    (1, 1, 1),
)
STEP = 0.01
EARLY_UNROLL, LATE_UNROLL = 8, 4
SOFTEN = 0.1
CELLS = 32
WIDE = CELLS + 4
ATOMS = 128
PAIRS = 16
NX, NY = 16, 4
LANES = 128
SEG = 40
ROW_LIVE, ROW_MIG, ROW_COUNT = 0, 1, 2
BEHIND = ((0, 0), (0, -1), (-1, 1), (-1, 0), (-1, -1))
NEAR = tuple((dx, dy) for dx in (-1, 0, 1) for dy in (-1, 0, 1))
MAX_TASKS = CELLS * PAIRS + len(BEHIND) * (CELLS + 2) * PAIRS

SMEM = pltpu.SMEM
VMEM = pltpu.VMEM
f32 = jnp.float32
bf16 = jnp.bfloat16
i32 = jnp.int32

OUT_T, AT_S, BUNDLE = 128, 144, 272
SPEEDS = 96
X1 = 3 * BUNDLE + 128 + SPEEDS
X2 = 384
SIZES = (BUNDLE, BUNDLE, BUNDLE, 128, X1, X1, X2, X2, SPEEDS, SPEEDS, SPEEDS)
P_B, P_OP, P_OM, P_O2, P_XP, P_XM, P_X2P, P_X2M, P_V, P_VP, P_VM, POOL = (
    sum(SIZES[:n]) for n in range(len(SIZES) + 1)
)


def column_rows():
    out = {(0, 0): P_B, (0, 1): P_OP, (0, -1): P_OM}
    for dx, x1, x2 in ((1, P_XP, P_X2P), (-1, P_XM, P_X2M)):
        out[dx, 0], out[dx, 1], out[dx, -1] = x1, x1 + BUNDLE, x1 + 2 * BUNDLE
        for n, dy in enumerate((0, 1, -1)):
            out[2 * dx, dy] = x2 + n * 128
    stay = {c: at + AT_S for c, at in out.items() if abs(c[0]) < 2}
    for dy in (-2, 2):
        out[0, dy] = P_O2
        for dx, x1 in ((1, P_XP), (-1, P_XM)):
            out[dx, dy] = x1 + 3 * BUNDLE
    return out, stay


OUT_AT, STAY_AT = column_rows()
FAR = tuple(c for c in ((0, 2), (1, 2), (-1, 2), (2, 0), (2, 1), (2, -1), (-2, 0), (-2, 1), (-2, -1)))
E_T = 16 * len(NEAR) + 8 * len(FAR)
E_V = E_T + 16
EDGE = E_V + 8
EDGE_AT = {c: 16 * n for n, c in enumerate(NEAR)}
for _n, _c in enumerate(FAR):
    EDGE_AT[_c] = 16 * len(NEAR) + 8 * _n - 8
    if _c[1] == 2:
        EDGE_AT[_c[0], -2] = EDGE_AT[_c]


def moved_by(array, axis, by):
    size = lax.axis_size(axis)
    return lax.ppermute(array, axis, [(i, (i + by) % size) for i in range(size)])


def to_column(rows):
    pad = jnp.zeros((LANES - rows.shape[0], LANES), f32)
    return jnp.concatenate([rows, pad], axis=0).T


def pack_kernel(*refs):
    sources, (bundle, alone, speeds), held, sems = refs[:8], refs[8:11], refs[11:19], refs[19]
    copies = [pltpu.make_async_copy(a, b, sems.at[n]) for n, (a, b) in enumerate(zip(sources, held))]
    for copy in copies:
        copy.start()
    for copy in copies:
        copy.wait()
    pos, stren, vel, first, second, live, mig, count = held
    bundle[OUT_T : OUT_T + 16, :] = jnp.zeros((16, LANES), f32)
    bundle[OUT_T : OUT_T + 16, 2 : 2 + CELLS] = first[...].astype(f32)
    bundle[OUT_T : OUT_T + 16, SEG + 2 : SEG + 2 + CELLS] = second[...].astype(f32)
    low = 2 * SEG + 2
    for row, ref in ((ROW_LIVE, live), (ROW_MIG, mig), (ROW_COUNT, count)):
        bundle[OUT_T + row : OUT_T + row + 1, low : low + CELLS] = ref[...].astype(f32)
    turned = to_column(bundle[OUT_T : OUT_T + 8, :])[low : low + CELLS, :]
    ids = jnp.broadcast_to(turned[:, ROW_MIG : ROW_MIG + 1], (CELLS, LANES))
    many = jnp.broadcast_to(turned[:, ROW_COUNT : ROW_COUNT + 1], (CELLS, LANES))
    low_slot = ids == 0.0
    kept = (1.0 - ids) < many
    filled = ids < many
    for c in range(4):
        if c < 3:
            one = pos[pl.ds(2 * c, CELLS, stride=6), :]
            two = pos[pl.ds(2 * c + 1, CELLS, stride=6), :]
        else:
            one = stren[pl.ds(0, CELLS, stride=2), :]
            two = stren[pl.ds(1, CELLS, stride=2), :]
        stay = jnp.where(kept, jnp.where(low_slot, two, one), 0.0)
        out = jnp.where(filled, jnp.where(low_slot, one, two), 0.0)
        bundle[pl.ds(AT_S + c, CELLS, stride=4), :] = stay
        bundle[pl.ds(c, CELLS, stride=4), :] = out
        alone[pl.ds(c, CELLS, stride=4), :] = out
    for c in range(3):
        one = vel[pl.ds(2 * c, CELLS, stride=6), :]
        two = vel[pl.ds(2 * c + 1, CELLS, stride=6), :]
        speed = jnp.where(filled, jnp.where(low_slot, one, two), 0.0)
        speeds[pl.ds(c, CELLS, stride=3), :] = speed


def place():
    return lax.axis_index("gx"), lax.axis_index("gy"), lax.axis_index("gz")


def heading_row(dest, x, y, dx, dy):
    row = lax.rem(x + (dx + NX), NX) * NY + lax.rem(y + (dy + NY), NY)
    return dest[pl.ds(row, 1), :]


def z_shift(z):
    return lax.rem(LANES + 2 - z * CELLS, LANES)


def iota(shape, axis):
    return lax.broadcasted_iota(i32, shape, axis)


def edges_kernel(b, op, om, o2, xp, xm, x2p, x2m, speeds, low, high):
    parts = (
        (P_B, b), (P_OP, op), (P_OM, om), (P_O2, o2),
        (P_XP, xp), (P_XM, xm), (P_X2P, x2p), (P_X2M, x2m),
    )

    def find(row):
        for start, ref in reversed(parts):
            if row >= start:
                return ref, row - start

    lane = iota((16, LANES), 1)
    for side, ref, cell in ((0, low, 0), (1, high, CELLS - 2)):
        table = jnp.zeros((16, LANES), f32)
        for n, column in enumerate(NEAR):
            source, row = find(OUT_AT[column])
            to = EDGE_AT[column]
            first = row + AT_S + 4 * cell
            ref[to : to + 8, :] = source[first : first + 8, :]
            ref[to + 8 : to + 16, :] = source[row + 4 * cell : row + 4 * cell + 8, :]
            values = source[row + OUT_T : row + OUT_T + 16, :]
            rolled = pltpu.roll(values, (2 * n - 2 - cell) % LANES, 1)
            for s in range(3):
                here = (lane >= s * SEG + 2 * n) & (lane < s * SEG + 2 * n + 2)
                table = jnp.where(here, rolled, table)
        for column in FAR:
            source, row = find(OUT_AT[column])
            to = EDGE_AT[column] + 8
            ref[to : to + 8, :] = source[row + 4 * cell : row + 4 * cell + 8, :]
        ref[E_T : E_T + 16, :] = table
        at = 88 if side else 0
        ref[E_V : E_V + 8, :] = speeds[at : at + 8, :]


def find_tasks(dest, near_tables, edges, masks, words, heads, occ, turn):
    x, y, z = place()
    heads[...] = jnp.zeros_like(heads)
    for dx in range(-2, 3):
        for dy in range(-2, 3):
            if abs(dx) + abs(dy) < 4:
                at = (dx + 2) * 5 + dy + 2
                heads[at : at + 1, :] = heading_row(dest, x, y, dx, dy)
    heads[...] = pltpu.roll(heads[...], z_shift(z), 1)

    def head(dx, dy):
        at = (dx + 2) * 5 + dy + 2
        return heads[at : at + 1, :]

    slot = iota((PAIRS, LANES), 0)
    lane = iota((PAIRS, LANES), 1)
    thin = iota((1, LANES), 1)
    tables = {}
    for n, column in enumerate(NEAR):
        ref, row = near_tables[column]
        values = ref[row : row + 16, :]
        if edges is not None:
            zlo, zhi = edges
            below = pltpu.roll(zlo[E_T : E_T + 16, :], (-2 * n) % LANES, 1)
            above = pltpu.roll(zhi[E_T : E_T + 16, :], (34 - 2 * n) % LANES, 1)
            for s in range(3):
                values = jnp.where((lane >= s * SEG) & (lane < s * SEG + 2), below, values)
                values = jnp.where((lane >= s * SEG + 34) & (lane < s * SEG + 36), above, values)
        tables[column] = values.astype(i32)
    rest = {c: pltpu.roll(tables[c], LANES - 2 * SEG, 1) for c in NEAR}
    ids = {c: rest[c][ROW_MIG : ROW_MIG + 1, :] for c in NEAR}
    counts = {c: rest[c][ROW_COUNT : ROW_COUNT + 1, :] for c in NEAR}
    filled = {c: (ids[c] < counts[c]).astype(i32) for c in NEAR}
    if edges is None:
        default = ((thin >= 2) & (thin < CELLS + 2)).astype(i32)
    else:
        default = jnp.ones((1, LANES), i32)

    def coming(dx, dy, face):
        return (head(dx, dy) == face).astype(i32) * filled.get((dx, dy), default)

    occ[...] = jnp.zeros_like(occ)
    turn[...] = jnp.zeros_like(turn)
    for n, (dx, dy) in enumerate(NEAR):
        turn[n : n + 1, :] = coming(dx, dy, 4) * 64
        turn[16 + n : 17 + n, :] = coming(dx, dy, 5) * 128
    from_below = pltpu.roll(turn[0:16, :], 1, 1)
    from_above = pltpu.roll(turn[16:32, :], LANES - 1, 1)
    for n, (dx, dy) in enumerate(NEAR):
        c = (dx, dy)
        kept0 = ((counts[c] > 0) & (ids[c] != 0)).astype(i32)
        kept1 = ((counts[c] > 1) & (ids[c] != 1)).astype(i32)
        sides = (
            coming(dx - 1, dy, 0) * 4
            + coming(dx + 1, dy, 1) * 8
            + coming(dx, dy - 1, 2) * 16
            + coming(dx, dy + 1, 3) * 32
        )
        occ[n : n + 1, :] = kept0 + 2 * kept1 + sides
    here = occ[...] + from_below + from_above
    by_z = {0: here, 1: pltpu.roll(here, LANES - 1, 1), -1: pltpu.roll(here, 1, 1)}

    def occupied(column, dz):
        n = NEAR.index(column)
        return jnp.broadcast_to(by_z[dz][n : n + 1, :], (PAIRS, LANES))

    def face_of(k):
        fx = jnp.where(k == 3, 1, jnp.where(k == 2, -1, 0))
        fy = jnp.where(k == 5, 1, jnp.where(k == 4, -1, 0))
        fz = jnp.where(k == 7, 1, jnp.where(k == 6, -1, 0))
        return fx, fy, fz

    def word_of(mine, target, theirs, at, vx, vy, vz, columns):
        half = (theirs >= 2).astype(i32)
        which = (vx + 2) * 5 + vy + 2
        inner = jnp.zeros_like(slot)
        outer = jnp.zeros_like(slot)
        stays = jnp.zeros_like(slot)
        for cx, cy in columns:
            same = which == (cx + 2) * 5 + cy + 2
            inner = jnp.where(same, OUT_AT[cx, cy] // 4, inner)
            if (cx, cy) in STAY_AT:
                stays = jnp.where(same, STAY_AT[cx, cy] // 4, stays)
            if edges is not None:
                outer = jnp.where(same, EDGE_AT[cx, cy] // 4, outer)
        entry = jnp.where(half == 1, inner, stays) + at - 2
        if edges is not None:
            low_edge = outer + 2 * half + at + POOL // 4
            high_edge = outer + 2 * half + at - 34 + (POOL + EDGE) // 4
            entry = jnp.where(at < 2, low_edge, jnp.where(at >= CELLS + 2, high_edge, entry))
        return (
            entry
            + (target * 8 + mine) * 2048
            + ((vx + 2) + 8 * (vy + 2) + 64 * (vz + 2)) * (2048 * 256)
        )

    masks[...] = jnp.zeros_like(masks)
    power = lax.shift_left(jnp.ones_like(slot), slot)
    for g, column in enumerate(BEHIND):
        cx, cy = column
        inside = lane < WIDE
        first = jnp.where(inside, tables[column], 0)
        second = jnp.where(inside, pltpu.roll(tables[column], LANES - SEG, 1), 0)
        live = inside & (slot < rest[column][ROW_LIVE : ROW_LIVE + 1, :])
        block = lax.shift_right_logical(second, 3)
        part = second & 7
        there = live & ((lax.shift_right_logical(occupied(column, 0), first) & 1) == 1)
        if g == 0:
            left = jnp.zeros((PAIRS, LANES), i32)
            bx, by, bz = left, left, left
            for b, (ox, oy, oz) in enumerate(SHELL):
                same = block == b
                bit = lax.shift_right_logical(occupied((ox, oy), oz), part) & 1
                left = jnp.where(same, bit, left)
                bx = jnp.where(same, ox, bx)
                by = jnp.where(same, oy, by)
                bz = jnp.where(same, oz, bz)
            keep = there & (left == 1) & (lane >= 2) & (lane < CELLS + 2)
            fx, fy, fz = face_of(part)
            found = [word_of(
                first, lane - 2, part, lane + bz + fz, bx + fx, by + fy, bz + fz, OUT_AT
            )]
            masks[0:1, :] = jnp.sum(jnp.where(keep, power, 0), axis=0, keepdims=True)
        right = jnp.zeros((PAIRS, LANES), i32)
        bz = right
        for b, (ox, oy, oz) in enumerate(SHELL):
            if (ox, oy) == (-cx, -cy):
                same = block == b
                bit = lax.shift_right_logical(occupied((0, 0), oz), part) & 1
                within = (lane + oz >= 2) & (lane + oz < CELLS + 2)
                right = jnp.where(same & within, bit, right)
                bz = jnp.where(same, oz, bz)
        keep = there & (right == 1) & (first != second)
        fx, fy, fz = face_of(first)
        columns = [(cx + a, cy + b) for a, b in ((0, 0), (1, 0), (-1, 0), (0, 1), (0, -1))]
        found.append(
            word_of(part, lane + bz - 2, first, lane + fz, cx + fx, cy + fy, fz - bz, columns)
        )
        masks[1 + g : 2 + g, :] = jnp.sum(jnp.where(keep, power, 0), axis=0, keepdims=True)
    masks[7:8, :] = jnp.sum(masks[0:6, :], axis=0, keepdims=True)
    for n in range(2):
        one, two, three = found[3 * n : 3 * n + 3]
        two, three = pltpu.roll(two, SEG, 1), pltpu.roll(three, 2 * SEG, 1)
        packed = jnp.where(lane < SEG, one, jnp.where(lane < 2 * SEG, two, three))
        words[PAIRS * n : PAIRS * (n + 1), :] = packed


def lowest_bit(mask):
    low = mask & -mask
    at = jnp.int32(0)
    for step, bits in ((8, 0xFF00), (4, 0xF0F0), (2, 0xCCCC), (1, 0xAAAA)):
        at = at + jnp.where((low & bits) != 0, step, 0)
    return at


def list_tasks(masks, words, spots, tasks, ready):
    many = jnp.int32(0)
    for lane in range(1, CELLS + 3):
        spots[many] = lane
        many = many + (masks[7, lane] != 0).astype(i32)

    def lane_step(s, n):
        lane = spots[s]
        for row in range(6):
            mask = masks[row, lane]
            spots[LANES + n] = mask
            spots[8 * LANES + n] = row // 3 * PAIRS * LANES + row % 3 * SEG + lane
            n = n + (mask != 0).astype(i32)
        return n

    found = lax.fori_loop(0, many, lane_step, jnp.int32(0))
    ready()

    def spot_step(s, n):
        spot = spots[8 * LANES + s]
        row = lax.shift_right_logical(spot, 7)
        lane = spot & (LANES - 1)

        def left(state):
            return state[0] != 0

        def take(state):
            mask, n = state
            tasks[n] = words[row + lowest_bit(mask), lane]
            return mask & (mask - 1), n + 1

        return lax.while_loop(left, take, take((spots[LANES + s], n)))[1]

    n = lax.fori_loop(0, found, spot_step, jnp.int32(0))
    for u in range(EARLY_UNROLL - 1):
        tasks[n + u] = 0
    return n


def extend(dest, pool, vel, ext, heads):
    x, y, z = place()
    heads[0:8, :] = jnp.zeros((8, LANES), i32)
    spots = ((-1, 0), (1, 0), (0, -1), (0, 1), (0, 0))
    for n, (dx, dy) in enumerate(spots):
        heads[n : n + 1, :] = heading_row(dest, x, y, dx, dy)
    turned = pltpu.roll(heads[0:8, :], z_shift(z), 1)
    heads[0:8, :] = turned
    heads[5:6, :] = pltpu.roll(turned, LANES - 1, 1)[4:5, :]
    heads[4:5, :] = pltpu.roll(turned, 1, 1)[4:5, :]
    valid = (heads[0:8, :] == iota((8, LANES), 0)).astype(f32)
    full = to_column(valid)
    turned = to_column(pool[P_B + OUT_T : P_B + OUT_T + 8, :])
    turned = turned[2 * SEG + 2 : 2 * SEG + 2 + CELLS, :]
    ids = jnp.broadcast_to(turned[:, ROW_MIG : ROW_MIG + 1], (CELLS, LANES))
    many = jnp.broadcast_to(turned[:, ROW_COUNT : ROW_COUNT + 1], (CELLS, LANES))
    for s in range(2):
        keep = (many > float(s)) & (ids != float(s))
        for r in range(7):
            if r < 3:
                value = pool[pl.ds(P_B + AT_S + r, CELLS, stride=4), :]
            elif r == 6:
                value = pool[pl.ds(P_B + AT_S + 3, CELLS, stride=4), :]
            else:
                value = vel[pl.ds(2 * (r - 3) + s, CELLS, stride=6), :]
            ext[pl.ds(8 * r + s, CELLS, stride=56), :] = jnp.where(keep, value, 0.0)
    places = (P_XM, P_XP, P_OM, P_OP, P_B, P_B)
    speeds = (P_XM + X1 - SPEEDS, P_XP + X1 - SPEEDS, P_VM, P_VP, P_V, P_V)
    for f in range(6):
        flag = jnp.broadcast_to(full[2 : 2 + CELLS, f : f + 1], (CELLS, LANES))
        for r in range(7):
            shift = float(FACES[f][r]) if r < 3 else 0.0
            if 3 <= r < 6:
                at, step = speeds[f] + r - 3, 3
            else:
                at, step = places[f] + min(r, 3), 4
            inner = CELLS - 1
            if f < 4:
                value = (pool[pl.ds(at, CELLS, stride=step), :] + shift) * flag
                ext[pl.ds(8 * r + 2 + f, CELLS, stride=56), :] = value
            elif f == 4:
                value = (pool[pl.ds(at, inner, stride=step), :] + shift) * flag[1:CELLS, :]
                ext[pl.ds(56 + 8 * r + 6, inner, stride=56), :] = value
                ext[8 * r + 6 : 8 * r + 7, :] = jnp.zeros((1, LANES), f32)
            else:
                value = (pool[pl.ds(at + step, inner, stride=step), :] + shift) * flag[0:inner, :]
                ext[pl.ds(8 * r + 7, inner, stride=56), :] = value
                last = 56 * inner + 8 * r + 7
                ext[last : last + 1, :] = jnp.zeros((1, LANES), f32)


def patch(dest, zlo, zhi, ext):
    x, y, z = place()
    rows = jnp.broadcast_to(heading_row(dest, x, y, 0, 0), (8, LANES))
    rows = pltpu.roll(rows, z_shift(z), 1)[0:1, :]
    thin = iota((1, LANES), 1)
    up = jnp.sum(jnp.where((thin == 1) & (rows == 4), 1.0, 0.0), axis=1, keepdims=True)
    down = jnp.sum(jnp.where((thin == CELLS + 2) & (rows == 5), 1.0, 0.0), axis=1, keepdims=True)
    for ref, flag, cell, slot, at, speed_at, shift in (
        (zlo, up, 0, 6, EDGE_AT[0, 0] + 12, E_V + 5, -1.0),
        (zhi, down, CELLS - 1, 7, EDGE_AT[0, 0] + 8, E_V, 1.0),
    ):
        for r in range(7):
            row = speed_at + r - 3 if 3 <= r < 6 else at + min(r, 3)
            value = (ref[row : row + 1, :] + (shift if r == 2 else 0.0)) * flag
            to = 56 * cell + 8 * r + slot
            ext[to : to + 1, :] = value


def inverse(value):
    return pl.reciprocal(value, approx=True)


def split(value):
    one = value.astype(bf16).astype(f32)
    rest = value - one
    two = rest.astype(bf16).astype(f32)
    return one, two, rest - two


def add_forces(tasks, many, pool, edges, ext, forces):
    unroll = EARLY_UNROLL if edges is None else LATE_UNROLL
    row = iota((8, LANES), 0)
    top = row < 4
    last = (row & 3) == 3

    def source_of(entry):
        near = pool[pl.ds(4 * jnp.minimum(entry, POOL // 4 - 1), 4), :]
        if edges is not None:
            which = jnp.maximum(entry - POOL // 4, 0)
            zlo, zhi = edges
            below = zlo[pl.ds(4 * jnp.minimum(which, EDGE // 4 - 1), 4), :]
            above = zhi[pl.ds(4 * jnp.maximum(which - EDGE // 4, 0), 4), :]
            near = jnp.where(entry < POOL // 4, near, jnp.where(which < EDGE // 4, below, above))
        return jnp.concatenate([near, near], axis=0)

    def length(value):
        return jnp.sum(jnp.where(top & ~last, value * value, 0.0), axis=0, keepdims=True)

    def one(code, live):
        entry = code & 2047
        target = lax.shift_right_logical(code, 11) & 255
        base = lax.shift_right_logical(target, 3) * 56 + (target & 7)
        away = lax.shift_right_logical(code, 19)
        raw = source_of(entry)
        source = jnp.where(last, raw, raw - 0.5)
        goal = jnp.zeros((8, LANES), f32)
        for a in range(3):
            shift = ((lax.shift_right_logical(away, 3 * a) & 7) - 2).astype(f32)
            wide = jnp.broadcast_to(ext[pl.ds(base + 8 * a, 1), :], (8, LANES))
            goal = jnp.where((row & 3) == a, wide - shift - 0.5, goal)
        strong = ext[pl.ds(base + 48, 1), :] * live
        s1, s2, s3 = split(source)
        t1, t2, t3 = split(goal)
        a1, a2, a3 = split(jnp.broadcast_to(-length(source), (8, LANES)))
        b1, b2, b3 = split(jnp.broadcast_to(1.0 - length(goal), (8, LANES)))
        w1, w2, w3 = 2.0 * s1, 2.0 * s2, 2.0 * s3
        left = jnp.concatenate(
            [
                jnp.where(last, jnp.where(top, a1, a2), jnp.where(top, w1, w2)),
                jnp.where(last, 1.0, jnp.where(top, w1, w2)),
                jnp.where(last, jnp.where(top, a3, 1.0), jnp.where(top, w1, w3)),
                jnp.zeros((8, LANES), f32),
            ],
            axis=0,
        ).astype(bf16)
        right = jnp.concatenate(
            [
                jnp.where(last, 1.0, t1),
                jnp.where(last, jnp.where(top, b1, b2), t2),
                jnp.where(last, jnp.where(top, 1.0, b3), jnp.where(top, t3, t1)),
                jnp.zeros((8, LANES), f32),
            ],
            axis=0,
        ).astype(bf16)
        inside = lax.dot_general(left, right, (((0,), (0,)), ((), ())), preferred_element_type=f32)
        reach = jnp.maximum(inside, 0.0)
        weight = reach * reach * inverse((1.0 + SOFTEN) - reach)
        high = weight.astype(bf16)
        low = (weight - high.astype(f32)).astype(bf16)
        gain = jnp.broadcast_to(raw[3:4, :], (8, LANES))
        v1, v2, v3 = split(jnp.where(last, gain, gain * source))
        moment = jnp.concatenate([jnp.where(top, v1, v2), jnp.where(top, v3, 0.0)], axis=0).astype(bf16)
        sums = jnp.dot(
            jnp.concatenate([moment, moment], axis=1),
            jnp.concatenate([high, low], axis=0),
            preferred_element_type=f32,
        )
        sums = sums[0:8, :] + sums[8:16, :]
        sums = sums[0:4, :] + sums[4:8, :]
        push = (goal[0:4, :] * sums[3:4, :] - sums) * strong
        to = lax.shift_right_logical(target, 3) * 24 + (target & 7)
        return to, push

    def step(t, _):
        at = unroll * t
        results = [one(tasks[at + u], (at + u < many).astype(f32)) for u in range(unroll)]
        for to, push in results:
            for a in range(3):
                forces[pl.ds(to + 8 * a, 1), :] += push[a : a + 1, :]
        return 0

    lax.fori_loop(0, lax.div(many + (unroll - 1), unroll), step, 0)


def to_scalars(masks, words, masks_s, words_s, sems):
    one = pltpu.make_async_copy(masks, masks_s, sems.at[0])
    two = pltpu.make_async_copy(words, words_s, sems.at[1])
    one.start()
    two.start()
    return one, two


def flags_kernel(dest, b, op, om, xp, xm, masks, words, heads, occ, turn):
    parts = ((P_B, b), (P_OP, op), (P_OM, om), (P_XP, xp), (P_XM, xm))
    tables = {}
    for column in NEAR:
        row = OUT_AT[column] + OUT_T
        start, ref = [part for part in parts if part[0] <= row][-1]
        tables[column] = (ref, row - start)
    find_tasks(dest, tables, None, masks, words, heads, occ, turn)


def early_kernel(
    dest, vel, pool, masks, words, ext, forces, heads, masks_s, words_s, spots, tasks, sems
):
    copies = to_scalars(masks, words, masks_s, words_s, sems)
    extend(dest, pool, vel, ext, heads)
    forces[...] = jnp.zeros_like(forces)
    copies[0].wait()
    many = list_tasks(masks_s, words_s, spots, tasks, copies[1].wait)
    add_forces(tasks, many, pool, None, ext, forces)


def late_kernel(
    dest, pool, zlo, zhi, ext_in, forces_in, done, moved, forces,
    ext, total, masks, words, occ, turn, heads, masks_s, words_s, spots, tasks, sems,
):
    tables = {c: (pool, OUT_AT[c] + OUT_T) for c in NEAR}
    find_tasks(dest, tables, (zlo, zhi), masks, words, heads, occ, turn)
    rest = masks[0:6, :] & ~done[0:6, :]
    masks[0:6, :] = rest
    masks[7:8, :] = jnp.sum(rest, axis=0, keepdims=True)
    copies = to_scalars(masks, words, masks_s, words_s, sems)
    ext[...] = ext_in[...]
    total[...] = forces_in[...]
    patch(dest, zlo, zhi, ext)
    copies[0].wait()
    many = list_tasks(masks_s, words_s, spots, tasks, copies[1].wait)
    add_forces(tasks, many, pool, (zlo, zhi), ext, total)

    def finish(cell, _):
        for a in range(3):
            force = total[pl.ds(pl.multiple_of(24 * cell + 8 * a, 8), 8), :]
            forces[0, 0, cell, a] = force
            speed = ext[pl.ds(pl.multiple_of(56 * cell + 24 + 8 * a, 8), 8), :] + STEP * force
            moved[0, 0, cell, 3 + a] = speed
            moved[0, 0, cell, a] = (
                ext[pl.ds(pl.multiple_of(56 * cell + 8 * a, 8), 8), :] + STEP * speed
            )
        return 0

    lax.fori_loop(0, CELLS, finish, 0)


def whole(space=VMEM):
    return pl.BlockSpec(memory_space=space)


def rows_of(n, dtype=f32):
    return jax.ShapeDtypeStruct((n, LANES), dtype)


def limit(mib):
    return pltpu.CompilerParams(vmem_limit_bytes=mib * 2**20)


WORDS = 2 * PAIRS
FIND_SCRATCH = [VMEM((16, LANES), i32), VMEM((32, LANES), i32)]
LIST_SCRATCH = [
    VMEM((32, LANES), i32),
    SMEM((8, LANES), i32),
    SMEM((WORDS, LANES), i32),
    SMEM((16 * LANES,), i32),
    SMEM((MAX_TASKS + 16,), i32),
    pltpu.SemaphoreType.DMA((2,)),
]


def copy_kernel(source, _, result):
    result[...] = source[...]


def held_back(array, other):
    return pl.pallas_call(
        copy_kernel,
        out_shape=rows_of(array.shape[0]),
        in_specs=[whole()] * 2,
        out_specs=whole(),
        cost_estimate=pl.CostEstimate(flops=20 * 10**9, bytes_accessed=2**20, transcendentals=0),
        compiler_params=limit(8),
        name="held",
    )(array, other[:8])


def per_device(
    positions,
    velocities,
    strength,
    cluster_count,
    migrant_ids,
    destination,
    pair_i,
    pair_j,
    pair_count,
):
    pos = positions.reshape((CELLS * 6, ATOMS))
    vel = velocities.reshape((CELLS * 6, ATOMS))
    stren = strength.reshape((CELLS * 2, ATOMS))
    dest = destination.reshape((NX * NY, LANES))
    B, O, V = pl.pallas_call(
        pack_kernel,
        out_shape=[rows_of(BUNDLE), rows_of(128), rows_of(SPEEDS)],
        in_specs=[whole(pltpu.HBM)] * 8,
        out_specs=[whole()] * 3,
        scratch_shapes=[
            VMEM((CELLS * 6, ATOMS), f32),
            VMEM((CELLS * 2, ATOMS), f32),
            VMEM((CELLS * 6, ATOMS), f32),
            VMEM((PAIRS, CELLS), i32),
            VMEM((PAIRS, CELLS), i32),
            VMEM((1, CELLS), i32),
            VMEM((1, CELLS), i32),
            VMEM((1, CELLS), i32),
            pltpu.SemaphoreType.DMA((8,)),
        ],
        compiler_params=limit(8),
        name="pack",
    )(
        *(
            pltpu.with_memory_space_constraint(a, pltpu.HBM)
            for a in (
                pos, stren, vel, pair_i[0, 0].T, pair_j[0, 0].T,
                pair_count.reshape((1, CELLS)), migrant_ids.reshape((1, CELLS)), cluster_count.reshape((1, CELLS)),
            )
        )
    )
    cat = jnp.concatenate
    O_2 = moved_by(O, "gy", 2)
    BV_p, B_m = moved_by(cat([B, V], axis=0), "gy", -1), moved_by(B, "gy", 1)
    B_p, V_p = BV_p[:BUNDLE], BV_p[BUNDLE:]
    near = cat([B, B_p, B_m, O_2, V], axis=0)
    far = cat([O, B_p[:128], B_m[:128]], axis=0)
    X_p, X_m = moved_by(near, "gx", -1), moved_by(near, "gx", 1)
    X2_p, X2_m = moved_by(far, "gx", -2), moved_by(far, "gx", 2)
    V_m = moved_by(held_back(V, B_p[:8] + B_m[:8] + O_2[:8]), "gy", 1)
    V_m = held_back(V_m, V_m)
    V_e = lax.optimization_barrier((V, V_m))[0]
    buffers = (B, B_p, B_m, O_2, X_p, X_m, X2_p, X2_m)
    low, high = pl.pallas_call(
        edges_kernel,
        out_shape=[rows_of(EDGE), rows_of(EDGE)],
        in_specs=[whole()] * 9,
        out_specs=[whole()] * 2,
        compiler_params=limit(8),
        name="edges",
    )(*buffers, V_e)
    zlo, zhi = moved_by(high, "gz", 1), moved_by(low, "gz", -1)
    masks, words = pl.pallas_call(
        flags_kernel,
        out_shape=[rows_of(8, i32), rows_of(WORDS, i32)],
        in_specs=[whole()] * 6,
        out_specs=[whole()] * 2,
        scratch_shapes=[VMEM((32, LANES), i32)] + FIND_SCRATCH,
        compiler_params=limit(8),
        name="flags",
    )(dest, B, B_p, B_m, X_p, X_m)
    pool = cat(buffers + (V, V_p, V_m), axis=0)
    ext, early = pl.pallas_call(
        early_kernel,
        out_shape=[rows_of(CELLS * 56), rows_of(CELLS * 24)],
        in_specs=[whole()] * 5,
        out_specs=[whole()] * 2,
        scratch_shapes=LIST_SCRATCH,
        compiler_params=limit(16),
        name="early",
    )(dest, vel, pool, masks, words)
    return pl.pallas_call(
        late_kernel,
        out_shape=[
            jax.ShapeDtypeStruct((1, 1, CELLS, 6, 8, LANES), f32),
            jax.ShapeDtypeStruct((1, 1, CELLS, 3, 8, LANES), f32),
        ],
        in_specs=[whole()] * 7,
        out_specs=[whole()] * 2,
        scratch_shapes=[
            VMEM((CELLS * 56, LANES), f32),
            VMEM((CELLS * 24, LANES), f32),
            VMEM((8, LANES), i32),
            VMEM((WORDS, LANES), i32),
        ]
        + FIND_SCRATCH
        + LIST_SCRATCH,
        compiler_params=limit(16),
        name="late",
    )(dest, pool, zlo, zhi, ext, early, masks)


def solution(mesh):
    in_specs = (
        P("gx", "gy", "gz", None, None, None),
        P("gx", "gy", "gz", None, None, None),
        P("gx", "gy", "gz", None, None),
        P("gx", "gy", "gz"),
        P("gx", "gy", "gz", None),
        P(),
        P("gx", "gy", "gz", None),
        P("gx", "gy", "gz", None),
        P("gx", "gy", "gz"),
    )
    out_specs = (P("gx", "gy", "gz", None, None, None), P("gx", "gy", "gz", None, None, None))
    return jax.shard_map(
        per_device, mesh=mesh, in_specs=in_specs, out_specs=out_specs, check_vma=False
    )
```

```python
import numpy as np
import jax
import jax.numpy as jnp
from jax import lax
from jax.experimental import pallas as pl
from jax.experimental.pallas import tpu as pltpu
from jax.sharding import PartitionSpec as P

FACES = ((-1, 0, 0), (1, 0, 0), (0, -1, 0), (0, 1, 0), (0, 0, -1), (0, 0, 1))
SHELL = (
    (0, 0, 0),
    (0, 0, 1),
    (0, 1, -1),
    (0, 1, 0),
    (0, 1, 1),
    (1, -1, -1),
    (1, -1, 0),
    (1, -1, 1),
    (1, 0, -1),
    (1, 0, 0),
    (1, 0, 1),
    (1, 1, -1),
    (1, 1, 0),
    (1, 1, 1),
)
STEP = 0.01
EARLY_UNROLL, LATE_UNROLL = 8, 4
SOFTEN = 0.1
CELLS = 32
WIDE = CELLS + 4
ATOMS = 128
PAIRS = 16
NX, NY = 16, 4
LANES = 128
SEG = 40
ROW_LIVE, ROW_MIG, ROW_COUNT = 0, 1, 2
BEHIND = ((0, 0), (0, -1), (-1, 1), (-1, 0), (-1, -1))
NEAR = tuple((dx, dy) for dx in (-1, 0, 1) for dy in (-1, 0, 1))
MAX_TASKS = CELLS * PAIRS + len(BEHIND) * (CELLS + 2) * PAIRS

SMEM = pltpu.SMEM
VMEM = pltpu.VMEM
f32 = jnp.float32
bf16 = jnp.bfloat16
i32 = jnp.int32

OUT_T, AT_S, BUNDLE = 128, 144, 272
SPEEDS = 96
X1 = 3 * BUNDLE + 128 + SPEEDS
X2 = 384
SIZES = (BUNDLE, BUNDLE, BUNDLE, 128, X1, X1, X2, X2, SPEEDS, SPEEDS, SPEEDS)
P_B, P_OP, P_OM, P_O2, P_XP, P_XM, P_X2P, P_X2M, P_V, P_VP, P_VM, POOL = (
    sum(SIZES[:n]) for n in range(len(SIZES) + 1)
)


def column_rows():
    out = {(0, 0): P_B, (0, 1): P_OP, (0, -1): P_OM}
    for dx, x1, x2 in ((1, P_XP, P_X2P), (-1, P_XM, P_X2M)):
        out[dx, 0], out[dx, 1], out[dx, -1] = x1, x1 + BUNDLE, x1 + 2 * BUNDLE
        for n, dy in enumerate((0, 1, -1)):
            out[2 * dx, dy] = x2 + n * 128
    stay = {c: at + AT_S for c, at in out.items() if abs(c[0]) < 2}
    for dy in (-2, 2):
        out[0, dy] = P_O2
        for dx, x1 in ((1, P_XP), (-1, P_XM)):
            out[dx, dy] = x1 + 3 * BUNDLE
    return out, stay


OUT_AT, STAY_AT = column_rows()
FAR = tuple(c for c in ((0, 2), (1, 2), (-1, 2), (2, 0), (2, 1), (2, -1), (-2, 0), (-2, 1), (-2, -1)))
E_T = 16 * len(NEAR) + 8 * len(FAR)
E_V = E_T + 16
EDGE = E_V + 8
EDGE_AT = {c: 16 * n for n, c in enumerate(NEAR)}
for _n, _c in enumerate(FAR):
    EDGE_AT[_c] = 16 * len(NEAR) + 8 * _n - 8
    if _c[1] == 2:
        EDGE_AT[_c[0], -2] = EDGE_AT[_c]


def moved_by(array, axis, by):
    size = lax.axis_size(axis)
    return lax.ppermute(array, axis, [(i, (i + by) % size) for i in range(size)])


def to_column(rows):
    pad = jnp.zeros((LANES - rows.shape[0], LANES), f32)
    return jnp.concatenate([rows, pad], axis=0).T


def pack_kernel(*refs):
    sources, (bundle, alone, speeds), held, sems = refs[:8], refs[8:11], refs[11:19], refs[19]
    copies = [pltpu.make_async_copy(a, b, sems.at[n]) for n, (a, b) in enumerate(zip(sources, held))]
    for copy in copies:
        copy.start()
    for copy in copies:
        copy.wait()
    pos, stren, vel, first, second, live, mig, count = held
    bundle[OUT_T : OUT_T + 16, :] = jnp.zeros((16, LANES), f32)
    bundle[OUT_T : OUT_T + 16, 2 : 2 + CELLS] = first[...].astype(f32)
    bundle[OUT_T : OUT_T + 16, SEG + 2 : SEG + 2 + CELLS] = second[...].astype(f32)
    low = 2 * SEG + 2
    for row, ref in ((ROW_LIVE, live), (ROW_MIG, mig), (ROW_COUNT, count)):
        bundle[OUT_T + row : OUT_T + row + 1, low : low + CELLS] = ref[...].astype(f32)
    turned = to_column(bundle[OUT_T : OUT_T + 8, :])[low : low + CELLS, :]
    ids = jnp.broadcast_to(turned[:, ROW_MIG : ROW_MIG + 1], (CELLS, LANES))
    many = jnp.broadcast_to(turned[:, ROW_COUNT : ROW_COUNT + 1], (CELLS, LANES))
    low_slot = ids == 0.0
    kept = (1.0 - ids) < many
    filled = ids < many
    for c in range(4):
        if c < 3:
            one = pos[pl.ds(2 * c, CELLS, stride=6), :]
            two = pos[pl.ds(2 * c + 1, CELLS, stride=6), :]
        else:
            one = stren[pl.ds(0, CELLS, stride=2), :]
            two = stren[pl.ds(1, CELLS, stride=2), :]
        stay = jnp.where(kept, jnp.where(low_slot, two, one), 0.0)
        out = jnp.where(filled, jnp.where(low_slot, one, two), 0.0)
        bundle[pl.ds(AT_S + c, CELLS, stride=4), :] = stay
        bundle[pl.ds(c, CELLS, stride=4), :] = out
        alone[pl.ds(c, CELLS, stride=4), :] = out
    for c in range(3):
        one = vel[pl.ds(2 * c, CELLS, stride=6), :]
        two = vel[pl.ds(2 * c + 1, CELLS, stride=6), :]
        speed = jnp.where(filled, jnp.where(low_slot, one, two), 0.0)
        speeds[pl.ds(c, CELLS, stride=3), :] = speed


def place():
    return lax.axis_index("gx"), lax.axis_index("gy"), lax.axis_index("gz")


def heading_row(dest, x, y, dx, dy):
    row = lax.rem(x + (dx + NX), NX) * NY + lax.rem(y + (dy + NY), NY)
    return dest[pl.ds(row, 1), :]


def z_shift(z):
    return lax.rem(LANES + 2 - z * CELLS, LANES)


def iota(shape, axis):
    return lax.broadcasted_iota(i32, shape, axis)


def edges_kernel(b, op, om, o2, xp, xm, x2p, x2m, speeds, low, high):
    parts = (
        (P_B, b), (P_OP, op), (P_OM, om), (P_O2, o2),
        (P_XP, xp), (P_XM, xm), (P_X2P, x2p), (P_X2M, x2m),
    )

    def find(row):
        for start, ref in reversed(parts):
            if row >= start:
                return ref, row - start

    lane = iota((16, LANES), 1)
    for side, ref, cell in ((0, low, 0), (1, high, CELLS - 2)):
        table = jnp.zeros((16, LANES), f32)
        for n, column in enumerate(NEAR):
            source, row = find(OUT_AT[column])
            to = EDGE_AT[column]
            first = row + AT_S + 4 * cell
            ref[to : to + 8, :] = source[first : first + 8, :]
            ref[to + 8 : to + 16, :] = source[row + 4 * cell : row + 4 * cell + 8, :]
            values = source[row + OUT_T : row + OUT_T + 16, :]
            rolled = pltpu.roll(values, (2 * n - 2 - cell) % LANES, 1)
            for s in range(3):
                here = (lane >= s * SEG + 2 * n) & (lane < s * SEG + 2 * n + 2)
                table = jnp.where(here, rolled, table)
        for column in FAR:
            source, row = find(OUT_AT[column])
            to = EDGE_AT[column] + 8
            ref[to : to + 8, :] = source[row + 4 * cell : row + 4 * cell + 8, :]
        ref[E_T : E_T + 16, :] = table
        at = 88 if side else 0
        ref[E_V : E_V + 8, :] = speeds[at : at + 8, :]


def find_tasks(dest, near_tables, edges, masks, words, heads, occ, turn):
    x, y, z = place()
    heads[...] = jnp.zeros_like(heads)
    for dx in range(-2, 3):
        for dy in range(-2, 3):
            if abs(dx) + abs(dy) < 4:
                at = (dx + 2) * 5 + dy + 2
                heads[at : at + 1, :] = heading_row(dest, x, y, dx, dy)
    heads[...] = pltpu.roll(heads[...], z_shift(z), 1)

    def head(dx, dy):
        at = (dx + 2) * 5 + dy + 2
        return heads[at : at + 1, :]

    slot = iota((PAIRS, LANES), 0)
    lane = iota((PAIRS, LANES), 1)
    thin = iota((1, LANES), 1)
    tables = {}
    for n, column in enumerate(NEAR):
        ref, row = near_tables[column]
        values = ref[row : row + 16, :]
        if edges is not None:
            zlo, zhi = edges
            below = pltpu.roll(zlo[E_T : E_T + 16, :], (-2 * n) % LANES, 1)
            above = pltpu.roll(zhi[E_T : E_T + 16, :], (34 - 2 * n) % LANES, 1)
            for s in range(3):
                values = jnp.where((lane >= s * SEG) & (lane < s * SEG + 2), below, values)
                values = jnp.where((lane >= s * SEG + 34) & (lane < s * SEG + 36), above, values)
        tables[column] = values.astype(i32)
    rest = {c: pltpu.roll(tables[c], LANES - 2 * SEG, 1) for c in NEAR}
    ids = {c: rest[c][ROW_MIG : ROW_MIG + 1, :] for c in NEAR}
    counts = {c: rest[c][ROW_COUNT : ROW_COUNT + 1, :] for c in NEAR}
    filled = {c: (ids[c] < counts[c]).astype(i32) for c in NEAR}
    if edges is None:
        default = ((thin >= 2) & (thin < CELLS + 2)).astype(i32)
    else:
        default = jnp.ones((1, LANES), i32)

    def coming(dx, dy, face):
        return (head(dx, dy) == face).astype(i32) * filled.get((dx, dy), default)

    occ[...] = jnp.zeros_like(occ)
    turn[...] = jnp.zeros_like(turn)
    for n, (dx, dy) in enumerate(NEAR):
        turn[n : n + 1, :] = coming(dx, dy, 4) * 64
        turn[16 + n : 17 + n, :] = coming(dx, dy, 5) * 128
    from_below = pltpu.roll(turn[0:16, :], 1, 1)
    from_above = pltpu.roll(turn[16:32, :], LANES - 1, 1)
    for n, (dx, dy) in enumerate(NEAR):
        c = (dx, dy)
        kept0 = ((counts[c] > 0) & (ids[c] != 0)).astype(i32)
        kept1 = ((counts[c] > 1) & (ids[c] != 1)).astype(i32)
        sides = (
            coming(dx - 1, dy, 0) * 4
            + coming(dx + 1, dy, 1) * 8
            + coming(dx, dy - 1, 2) * 16
            + coming(dx, dy + 1, 3) * 32
        )
        occ[n : n + 1, :] = kept0 + 2 * kept1 + sides
    here = occ[...] + from_below + from_above
    by_z = {0: here, 1: pltpu.roll(here, LANES - 1, 1), -1: pltpu.roll(here, 1, 1)}

    def occupied(column, dz):
        n = NEAR.index(column)
        return jnp.broadcast_to(by_z[dz][n : n + 1, :], (PAIRS, LANES))

    def face_of(k):
        fx = jnp.where(k == 3, 1, jnp.where(k == 2, -1, 0))
        fy = jnp.where(k == 5, 1, jnp.where(k == 4, -1, 0))
        fz = jnp.where(k == 7, 1, jnp.where(k == 6, -1, 0))
        return fx, fy, fz

    def word_of(mine, target, theirs, at, vx, vy, vz, columns):
        half = (theirs >= 2).astype(i32)
        which = (vx + 2) * 5 + vy + 2
        inner = jnp.zeros_like(slot)
        outer = jnp.zeros_like(slot)
        stays = jnp.zeros_like(slot)
        for cx, cy in columns:
            same = which == (cx + 2) * 5 + cy + 2
            inner = jnp.where(same, OUT_AT[cx, cy] // 4, inner)
            if (cx, cy) in STAY_AT:
                stays = jnp.where(same, STAY_AT[cx, cy] // 4, stays)
            if edges is not None:
                outer = jnp.where(same, EDGE_AT[cx, cy] // 4, outer)
        entry = jnp.where(half == 1, inner, stays) + at - 2
        if edges is not None:
            low_edge = outer + 2 * half + at + POOL // 4
            high_edge = outer + 2 * half + at - 34 + (POOL + EDGE) // 4
            entry = jnp.where(at < 2, low_edge, jnp.where(at >= CELLS + 2, high_edge, entry))
        return (
            entry
            + (target * 8 + mine) * 2048
            + ((vx + 2) + 8 * (vy + 2) + 64 * (vz + 2)) * (2048 * 256)
        )

    masks[...] = jnp.zeros_like(masks)
    power = lax.shift_left(jnp.ones_like(slot), slot)
    for g, column in enumerate(BEHIND):
        cx, cy = column
        inside = lane < WIDE
        first = jnp.where(inside, tables[column], 0)
        second = jnp.where(inside, pltpu.roll(tables[column], LANES - SEG, 1), 0)
        live = inside & (slot < rest[column][ROW_LIVE : ROW_LIVE + 1, :])
        block = lax.shift_right_logical(second, 3)
        part = second & 7
        there = live & ((lax.shift_right_logical(occupied(column, 0), first) & 1) == 1)
        if g == 0:
            left = jnp.zeros((PAIRS, LANES), i32)
            bx, by, bz = left, left, left
            for b, (ox, oy, oz) in enumerate(SHELL):
                same = block == b
                bit = lax.shift_right_logical(occupied((ox, oy), oz), part) & 1
                left = jnp.where(same, bit, left)
                bx = jnp.where(same, ox, bx)
                by = jnp.where(same, oy, by)
                bz = jnp.where(same, oz, bz)
            keep = there & (left == 1) & (lane >= 2) & (lane < CELLS + 2)
            fx, fy, fz = face_of(part)
            found = [word_of(
                first, lane - 2, part, lane + bz + fz, bx + fx, by + fy, bz + fz, OUT_AT
            )]
            masks[0:1, :] = jnp.sum(jnp.where(keep, power, 0), axis=0, keepdims=True)
        right = jnp.zeros((PAIRS, LANES), i32)
        bz = right
        for b, (ox, oy, oz) in enumerate(SHELL):
            if (ox, oy) == (-cx, -cy):
                same = block == b
                bit = lax.shift_right_logical(occupied((0, 0), oz), part) & 1
                within = (lane + oz >= 2) & (lane + oz < CELLS + 2)
                right = jnp.where(same & within, bit, right)
                bz = jnp.where(same, oz, bz)
        keep = there & (right == 1) & (first != second)
        fx, fy, fz = face_of(first)
        columns = [(cx + a, cy + b) for a, b in ((0, 0), (1, 0), (-1, 0), (0, 1), (0, -1))]
        found.append(
            word_of(part, lane + bz - 2, first, lane + fz, cx + fx, cy + fy, fz - bz, columns)
        )
        masks[1 + g : 2 + g, :] = jnp.sum(jnp.where(keep, power, 0), axis=0, keepdims=True)
    masks[7:8, :] = jnp.sum(masks[0:6, :], axis=0, keepdims=True)
    for n in range(2):
        one, two, three = found[3 * n : 3 * n + 3]
        two, three = pltpu.roll(two, SEG, 1), pltpu.roll(three, 2 * SEG, 1)
        packed = jnp.where(lane < SEG, one, jnp.where(lane < 2 * SEG, two, three))
        words[PAIRS * n : PAIRS * (n + 1), :] = packed


def lowest_bit(mask):
    low = mask & -mask
    at = jnp.int32(0)
    for step, bits in ((8, 0xFF00), (4, 0xF0F0), (2, 0xCCCC), (1, 0xAAAA)):
        at = at + jnp.where((low & bits) != 0, step, 0)
    return at


def list_tasks(masks, words, spots, tasks, ready):
    many = jnp.int32(0)
    for lane in range(1, CELLS + 3):
        spots[many] = lane
        many = many + (masks[7, lane] != 0).astype(i32)

    def lane_step(s, n):
        lane = spots[s]
        for row in range(6):
            mask = masks[row, lane]
            spots[LANES + n] = mask
            spots[8 * LANES + n] = row // 3 * PAIRS * LANES + row % 3 * SEG + lane
            n = n + (mask != 0).astype(i32)
        return n

    found = lax.fori_loop(0, many, lane_step, jnp.int32(0))
    ready()

    def spot_step(s, n):
        spot = spots[8 * LANES + s]
        row = lax.shift_right_logical(spot, 7)
        lane = spot & (LANES - 1)

        def left(state):
            return state[0] != 0

        def take(state):
            mask, n = state
            tasks[n] = words[row + lowest_bit(mask), lane]
            return mask & (mask - 1), n + 1

        return lax.while_loop(left, take, take((spots[LANES + s], n)))[1]

    n = lax.fori_loop(0, found, spot_step, jnp.int32(0))
    for u in range(EARLY_UNROLL - 1):
        tasks[n + u] = 0
    return n


def extend(dest, pool, vel, ext, heads):
    x, y, z = place()
    heads[0:8, :] = jnp.zeros((8, LANES), i32)
    spots = ((-1, 0), (1, 0), (0, -1), (0, 1), (0, 0))
    for n, (dx, dy) in enumerate(spots):
        heads[n : n + 1, :] = heading_row(dest, x, y, dx, dy)
    turned = pltpu.roll(heads[0:8, :], z_shift(z), 1)
    heads[0:8, :] = turned
    heads[5:6, :] = pltpu.roll(turned, LANES - 1, 1)[4:5, :]
    heads[4:5, :] = pltpu.roll(turned, 1, 1)[4:5, :]
    valid = (heads[0:8, :] == iota((8, LANES), 0)).astype(f32)
    full = to_column(valid)
    turned = to_column(pool[P_B + OUT_T : P_B + OUT_T + 8, :])
    turned = turned[2 * SEG + 2 : 2 * SEG + 2 + CELLS, :]
    ids = jnp.broadcast_to(turned[:, ROW_MIG : ROW_MIG + 1], (CELLS, LANES))
    many = jnp.broadcast_to(turned[:, ROW_COUNT : ROW_COUNT + 1], (CELLS, LANES))
    for s in range(2):
        keep = (many > float(s)) & (ids != float(s))
        for r in range(7):
            if r < 3:
                value = pool[pl.ds(P_B + AT_S + r, CELLS, stride=4), :]
            elif r == 6:
                value = pool[pl.ds(P_B + AT_S + 3, CELLS, stride=4), :]
            else:
                value = vel[pl.ds(2 * (r - 3) + s, CELLS, stride=6), :]
            ext[pl.ds(8 * r + s, CELLS, stride=56), :] = jnp.where(keep, value, 0.0)
    places = (P_XM, P_XP, P_OM, P_OP, P_B, P_B)
    speeds = (P_XM + X1 - SPEEDS, P_XP + X1 - SPEEDS, P_VM, P_VP, P_V, P_V)
    for f in range(6):
        flag = jnp.broadcast_to(full[2 : 2 + CELLS, f : f + 1], (CELLS, LANES))
        for r in range(7):
            shift = float(FACES[f][r]) if r < 3 else 0.0
            if 3 <= r < 6:
                at, step = speeds[f] + r - 3, 3
            else:
                at, step = places[f] + min(r, 3), 4
            inner = CELLS - 1
            if f < 4:
                value = (pool[pl.ds(at, CELLS, stride=step), :] + shift) * flag
                ext[pl.ds(8 * r + 2 + f, CELLS, stride=56), :] = value
            elif f == 4:
                value = (pool[pl.ds(at, inner, stride=step), :] + shift) * flag[1:CELLS, :]
                ext[pl.ds(56 + 8 * r + 6, inner, stride=56), :] = value
                ext[8 * r + 6 : 8 * r + 7, :] = jnp.zeros((1, LANES), f32)
            else:
                value = (pool[pl.ds(at + step, inner, stride=step), :] + shift) * flag[0:inner, :]
                ext[pl.ds(8 * r + 7, inner, stride=56), :] = value
                last = 56 * inner + 8 * r + 7
                ext[last : last + 1, :] = jnp.zeros((1, LANES), f32)


def patch(dest, zlo, zhi, ext):
    x, y, z = place()
    rows = jnp.broadcast_to(heading_row(dest, x, y, 0, 0), (8, LANES))
    rows = pltpu.roll(rows, z_shift(z), 1)[0:1, :]
    thin = iota((1, LANES), 1)
    up = jnp.sum(jnp.where((thin == 1) & (rows == 4), 1.0, 0.0), axis=1, keepdims=True)
    down = jnp.sum(jnp.where((thin == CELLS + 2) & (rows == 5), 1.0, 0.0), axis=1, keepdims=True)
    for ref, flag, cell, slot, at, speed_at, shift in (
        (zlo, up, 0, 6, EDGE_AT[0, 0] + 12, E_V + 5, -1.0),
        (zhi, down, CELLS - 1, 7, EDGE_AT[0, 0] + 8, E_V, 1.0),
    ):
        for r in range(7):
            row = speed_at + r - 3 if 3 <= r < 6 else at + min(r, 3)
            value = (ref[row : row + 1, :] + (shift if r == 2 else 0.0)) * flag
            to = 56 * cell + 8 * r + slot
            ext[to : to + 1, :] = value


def inverse(value):
    return pl.reciprocal(value, approx=True)


def split(value):
    one = value.astype(bf16).astype(f32)
    rest = value - one
    two = rest.astype(bf16).astype(f32)
    return one, two, rest - two


def add_forces(tasks, many, pool, edges, ext, forces):
    unroll = EARLY_UNROLL if edges is None else LATE_UNROLL
    row = iota((8, LANES), 0)
    top = row < 4
    last = (row & 3) == 3

    def source_of(entry):
        near = pool[pl.ds(4 * jnp.minimum(entry, POOL // 4 - 1), 4), :]
        if edges is not None:
            which = jnp.maximum(entry - POOL // 4, 0)
            zlo, zhi = edges
            below = zlo[pl.ds(4 * jnp.minimum(which, EDGE // 4 - 1), 4), :]
            above = zhi[pl.ds(4 * jnp.maximum(which - EDGE // 4, 0), 4), :]
            near = jnp.where(entry < POOL // 4, near, jnp.where(which < EDGE // 4, below, above))
        return jnp.concatenate([near, near], axis=0)

    def length(value):
        return jnp.sum(jnp.where(top & ~last, value * value, 0.0), axis=0, keepdims=True)

    def one(code, live):
        entry = code & 2047
        target = lax.shift_right_logical(code, 11) & 255
        base = lax.shift_right_logical(target, 3) * 56 + (target & 7)
        away = lax.shift_right_logical(code, 19)
        raw = source_of(entry)
        source = jnp.where(last, raw, raw - 0.5)
        goal = jnp.zeros((8, LANES), f32)
        for a in range(3):
            shift = ((lax.shift_right_logical(away, 3 * a) & 7) - 2).astype(f32)
            wide = jnp.broadcast_to(ext[pl.ds(base + 8 * a, 1), :], (8, LANES))
            goal = jnp.where((row & 3) == a, wide - shift - 0.5, goal)
        strong = ext[pl.ds(base + 48, 1), :] * live
        s1, s2, s3 = split(source)
        t1, t2, t3 = split(goal)
        a1, a2, a3 = split(jnp.broadcast_to(-length(source), (8, LANES)))
        b1, b2, b3 = split(jnp.broadcast_to(1.0 - length(goal), (8, LANES)))
        w1, w2, w3 = 2.0 * s1, 2.0 * s2, 2.0 * s3
        left = jnp.concatenate(
            [
                jnp.where(last, jnp.where(top, a1, a2), jnp.where(top, w1, w2)),
                jnp.where(last, 1.0, jnp.where(top, w1, w2)),
                jnp.where(last, jnp.where(top, a3, 1.0), jnp.where(top, w1, w3)),
                jnp.zeros((8, LANES), f32),
            ],
            axis=0,
        ).astype(bf16)
        right = jnp.concatenate(
            [
                jnp.where(last, 1.0, t1),
                jnp.where(last, jnp.where(top, b1, b2), t2),
                jnp.where(last, jnp.where(top, 1.0, b3), jnp.where(top, t3, t1)),
                jnp.zeros((8, LANES), f32),
            ],
            axis=0,
        ).astype(bf16)
        inside = lax.dot_general(left, right, (((0,), (0,)), ((), ())), preferred_element_type=f32)
        reach = jnp.maximum(inside, 0.0)
        weight = reach * reach * inverse((1.0 + SOFTEN) - reach)
        high = weight.astype(bf16)
        low = (weight - high.astype(f32)).astype(bf16)
        gain = jnp.broadcast_to(raw[3:4, :], (8, LANES))
        v1, v2, v3 = split(jnp.where(last, gain, gain * source))
        moment = jnp.concatenate([jnp.where(top, v1, v2), jnp.where(top, v3, 0.0)], axis=0).astype(bf16)
        sums = jnp.dot(
            jnp.concatenate([moment, moment], axis=1),
            jnp.concatenate([high, low], axis=0),
            preferred_element_type=f32,
        )
        sums = sums[0:8, :] + sums[8:16, :]
        sums = sums[0:4, :] + sums[4:8, :]
        push = (goal[0:4, :] * sums[3:4, :] - sums) * strong
        to = lax.shift_right_logical(target, 3) * 24 + (target & 7)
        return to, push

    def step(t, _):
        at = unroll * t
        results = [one(tasks[at + u], (at + u < many).astype(f32)) for u in range(unroll)]
        for to, push in results:
            for a in range(3):
                forces[pl.ds(to + 8 * a, 1), :] += push[a : a + 1, :]
        return 0

    lax.fori_loop(0, lax.div(many + (unroll - 1), unroll), step, 0)


def to_scalars(masks, words, masks_s, words_s, sems):
    one = pltpu.make_async_copy(masks, masks_s, sems.at[0])
    two = pltpu.make_async_copy(words, words_s, sems.at[1])
    one.start()
    two.start()
    return one, two


def flags_kernel(dest, b, op, om, xp, xm, masks, words, heads, occ, turn):
    parts = ((P_B, b), (P_OP, op), (P_OM, om), (P_XP, xp), (P_XM, xm))
    tables = {}
    for column in NEAR:
        row = OUT_AT[column] + OUT_T
        start, ref = [part for part in parts if part[0] <= row][-1]
        tables[column] = (ref, row - start)
    find_tasks(dest, tables, None, masks, words, heads, occ, turn)


def early_kernel(
    dest, vel, pool, masks, words, ext, forces, heads, masks_s, words_s, spots, tasks, sems
):
    copies = to_scalars(masks, words, masks_s, words_s, sems)
    extend(dest, pool, vel, ext, heads)
    forces[...] = jnp.zeros_like(forces)
    copies[0].wait()
    many = list_tasks(masks_s, words_s, spots, tasks, copies[1].wait)
    add_forces(tasks, many, pool, None, ext, forces)


def late_kernel(
    dest, pool, zlo, zhi, ext_in, forces_in, done, moved, forces,
    ext, total, masks, words, occ, turn, heads, masks_s, words_s, spots, tasks, sems,
):
    tables = {c: (pool, OUT_AT[c] + OUT_T) for c in NEAR}
    find_tasks(dest, tables, (zlo, zhi), masks, words, heads, occ, turn)
    rest = masks[0:6, :] & ~done[0:6, :]
    masks[0:6, :] = rest
    masks[7:8, :] = jnp.sum(rest, axis=0, keepdims=True)
    copies = to_scalars(masks, words, masks_s, words_s, sems)
    ext[...] = ext_in[...]
    total[...] = forces_in[...]
    patch(dest, zlo, zhi, ext)
    copies[0].wait()
    many = list_tasks(masks_s, words_s, spots, tasks, copies[1].wait)
    add_forces(tasks, many, pool, (zlo, zhi), ext, total)

    def finish(cell, _):
        for a in range(3):
            force = total[pl.ds(pl.multiple_of(24 * cell + 8 * a, 8), 8), :]
            forces[0, 0, cell, a] = force
            speed = ext[pl.ds(pl.multiple_of(56 * cell + 24 + 8 * a, 8), 8), :] + STEP * force
            moved[0, 0, cell, 3 + a] = speed
            moved[0, 0, cell, a] = (
                ext[pl.ds(pl.multiple_of(56 * cell + 8 * a, 8), 8), :] + STEP * speed
            )
        return 0

    lax.fori_loop(0, CELLS, finish, 0)


def whole(space=VMEM):
    return pl.BlockSpec(memory_space=space)


def rows_of(n, dtype=f32):
    return jax.ShapeDtypeStruct((n, LANES), dtype)


def limit(mib):
    return pltpu.CompilerParams(vmem_limit_bytes=mib * 2**20)


WORDS = 2 * PAIRS
FIND_SCRATCH = [VMEM((16, LANES), i32), VMEM((32, LANES), i32)]
LIST_SCRATCH = [
    VMEM((32, LANES), i32),
    SMEM((8, LANES), i32),
    SMEM((WORDS, LANES), i32),
    SMEM((16 * LANES,), i32),
    SMEM((MAX_TASKS + 16,), i32),
    pltpu.SemaphoreType.DMA((2,)),
]


def copy_kernel(source, _, result):
    result[...] = source[...]


def held_back(array, other):
    return pl.pallas_call(
        copy_kernel,
        out_shape=rows_of(array.shape[0]),
        in_specs=[whole()] * 2,
        out_specs=whole(),
        cost_estimate=pl.CostEstimate(flops=20 * 10**9, bytes_accessed=2**20, transcendentals=0),
        compiler_params=limit(8),
        name="held",
    )(array, other[:8])


def per_device(
    positions,
    velocities,
    strength,
    cluster_count,
    migrant_ids,
    destination,
    pair_i,
    pair_j,
    pair_count,
):
    pos = positions.reshape((CELLS * 6, ATOMS))
    vel = velocities.reshape((CELLS * 6, ATOMS))
    stren = strength.reshape((CELLS * 2, ATOMS))
    dest = destination.reshape((NX * NY, LANES))
    B, O, V = pl.pallas_call(
        pack_kernel,
        out_shape=[rows_of(BUNDLE), rows_of(128), rows_of(SPEEDS)],
        in_specs=[whole(pltpu.HBM)] * 8,
        out_specs=[whole()] * 3,
        scratch_shapes=[
            VMEM((CELLS * 6, ATOMS), f32),
            VMEM((CELLS * 2, ATOMS), f32),
            VMEM((CELLS * 6, ATOMS), f32),
            VMEM((PAIRS, CELLS), i32),
            VMEM((PAIRS, CELLS), i32),
            VMEM((1, CELLS), i32),
            VMEM((1, CELLS), i32),
            VMEM((1, CELLS), i32),
            pltpu.SemaphoreType.DMA((8,)),
        ],
        compiler_params=limit(8),
        name="pack",
    )(
        *(
            pltpu.with_memory_space_constraint(a, pltpu.HBM)
            for a in (
                pos, stren, vel, pair_i[0, 0].T, pair_j[0, 0].T,
                pair_count.reshape((1, CELLS)), migrant_ids.reshape((1, CELLS)), cluster_count.reshape((1, CELLS)),
            )
        )
    )
    cat = jnp.concatenate
    O_2 = moved_by(O, "gy", 2)
    BV_p, B_m = moved_by(cat([B, V], axis=0), "gy", -1), moved_by(B, "gy", 1)
    B_p, V_p = BV_p[:BUNDLE], BV_p[BUNDLE:]
    near = cat([B, B_p, B_m, O_2, V], axis=0)
    far = cat([O, B_p[:128], B_m[:128]], axis=0)
    X_p, X_m = moved_by(near, "gx", -1), moved_by(near, "gx", 1)
    X2_p, X2_m = moved_by(far, "gx", -2), moved_by(far, "gx", 2)
    V_m = moved_by(held_back(V, B_p[:8] + B_m[:8] + O_2[:8]), "gy", 1)
    buffers = (B, B_p, B_m, O_2, X_p, X_m, X2_p, X2_m)
    low, high = pl.pallas_call(
        edges_kernel,
        out_shape=[rows_of(EDGE), rows_of(EDGE)],
        in_specs=[whole()] * 9,
        out_specs=[whole()] * 2,
        compiler_params=limit(8),
        name="edges",
    )(*buffers, V)
    zlo, zhi = moved_by(high, "gz", 1), moved_by(low, "gz", -1)
    masks, words = pl.pallas_call(
        flags_kernel,
        out_shape=[rows_of(8, i32), rows_of(WORDS, i32)],
        in_specs=[whole()] * 6,
        out_specs=[whole()] * 2,
        scratch_shapes=[VMEM((32, LANES), i32)] + FIND_SCRATCH,
        compiler_params=limit(8),
        name="flags",
    )(dest, B, B_p, B_m, X_p, X_m)
    pool = cat(buffers + (V, V_p, V_m), axis=0)
    ext, early = pl.pallas_call(
        early_kernel,
        out_shape=[rows_of(CELLS * 56), rows_of(CELLS * 24)],
        in_specs=[whole()] * 5,
        out_specs=[whole()] * 2,
        scratch_shapes=LIST_SCRATCH,
        compiler_params=limit(16),
        name="early",
    )(dest, vel, pool, masks, words)
    return pl.pallas_call(
        late_kernel,
        out_shape=[
            jax.ShapeDtypeStruct((1, 1, CELLS, 6, 8, LANES), f32),
            jax.ShapeDtypeStruct((1, 1, CELLS, 3, 8, LANES), f32),
        ],
        in_specs=[whole()] * 7,
        out_specs=[whole()] * 2,
        scratch_shapes=[
            VMEM((CELLS * 56, LANES), f32),
            VMEM((CELLS * 24, LANES), f32),
            VMEM((8, LANES), i32),
            VMEM((WORDS, LANES), i32),
        ]
        + FIND_SCRATCH
        + LIST_SCRATCH,
        compiler_params=limit(16),
        name="late",
    )(dest, pool, zlo, zhi, ext, early, masks)


def solution(mesh):
    in_specs = (
        P("gx", "gy", "gz", None, None, None),
        P("gx", "gy", "gz", None, None, None),
        P("gx", "gy", "gz", None, None),
        P("gx", "gy", "gz"),
        P("gx", "gy", "gz", None),
        P(),
        P("gx", "gy", "gz", None),
        P("gx", "gy", "gz", None),
        P("gx", "gy", "gz"),
    )
    out_specs = (P("gx", "gy", "gz", None, None, None), P("gx", "gy", "gz", None, None, None))
    return jax.shard_map(
        per_device, mesh=mesh, in_specs=in_specs, out_specs=out_specs, check_vma=False
    )
```
